32 devices in a mesh: snp: 8 (over y, x, core), samp: 4 (over z).
Axes of the slice: x: 2, y: 2, z: 4, core: 2. Of those that a mesh axis runs over, the one named last changes fastest.
Arguments:
- genotypes: float32 [8192, 2048], P('snp', 'samp'), may hold values from -1 to 2, as said below
- pcs: float32 [20, 2048], P(None, 'samp'), may hold values from -6 to 6
Outputs:
- kinship: float32 [2048, 2048], P('snp', 'samp')
The draws below stay inside these ranges and needn't reach their ends.
Inputs may be any that keep to these rules, and one draw needn't show every extreme that they name: `genotypes`: observed entries are real-valued dosages from 0 to 2 and -1 marks a missing entry; SNPs whose index is a multiple of 16 are never missing.
All inputs are finite; a program needn't handle non-finite values.
Results may differ from the reference program's by a relative error of at most 0.0015.
Values may be sent and summed in bfloat16 or wider, within the bound.
No kernel may reach another device: no remote copies, remote signals or barrier semaphores. Data moves between devices by JAX's collectives and lax.ppermute only.
A program may use at most 64 MiB of HBM per device.

```python
import jax
import jax.numpy as jnp
from jax import lax

K = 20
SNPS = 8192
N = 2048


population_groups = 6


family_members = 4


def families(key):
    order = jax.random.permutation(jax.random.fold_in(key, 5), N)
    return order // family_members


def population(key):
    family = families(key)
    family_groups = jax.random.randint(jax.random.fold_in(key, 7), (N // family_members,), 0, population_groups)
    return family_groups[family]


def allele_copy(key, salt, chosen, shared_allele):
    fresh = (jax.random.randint(jax.random.fold_in(key, salt), (SNPS, N), 0, 1000) < chosen).astype(jnp.int32)
    inherit = jax.random.randint(jax.random.fold_in(key, salt + 1), (SNPS, N), 0, 2) == 1
    return jnp.where(inherit, shared_allele, fresh)


def draw_genotypes(key, part):
    groups = population(key)
    family = families(key)
    limits = jax.random.randint(jax.random.fold_in(key, 11), (SNPS, population_groups), 1, 500)
    chosen = jnp.take(limits, groups, axis=1)
    family_chosen = jnp.take(limits, jax.random.randint(jax.random.fold_in(key, 7), (N // family_members,), 0, population_groups), axis=1)
    shared_first = (jax.random.randint(jax.random.fold_in(key, 31), (SNPS, N // family_members), 0, 1000) < family_chosen).astype(jnp.int32)
    shared_second = (jax.random.randint(jax.random.fold_in(key, 37), (SNPS, N // family_members), 0, 1000) < family_chosen).astype(jnp.int32)
    first = allele_copy(key, 13, chosen, jnp.take(shared_first, family, axis=1))
    second = allele_copy(key, 17, chosen, jnp.take(shared_second, family, axis=1))
    hard = (first + second).astype(jnp.float32)
    noise = jax.random.uniform(jax.random.fold_in(key, 41), (SNPS, N), jnp.float32, -0.45, 0.45)
    soft = jnp.clip(hard + noise, 0.0, 2.0)
    sample_rate = jax.random.randint(jax.random.fold_in(key, 43), (1, N), 0, 257)
    lost = jax.random.randint(jax.random.fold_in(key, 19), (SNPS, N), 0, 1024) < sample_rate
    snp_index = jnp.arange(SNPS)[:, None]
    lost = jnp.logical_and(lost, snp_index % 16 != 0)
    return jnp.where(lost, -1.0, soft).astype(jnp.float32)


def draw_pcs(key, part):
    groups = population(key)
    loadings = jax.random.normal(jax.random.fold_in(key, 21), (K, population_groups), jnp.float32)
    centers = jnp.take(loadings, groups, axis=1)
    noise = jax.random.normal(jax.random.fold_in(key, 23), (K, N), jnp.float32)
    values = centers + 0.5 * noise
    return jnp.clip(values, -6.0, 6.0).astype(jnp.float32)


def setup_inputs(seed: int = 0) -> dict:
    streams_of = jax.random.split(jax.random.key(seed), 3)
    return {
        "genotypes": draw_genotypes(jax.random.fold_in(streams_of[2], 71), 0),
        "pcs": draw_pcs(jax.random.fold_in(streams_of[2], 71), 0),
    }


def reference(genotypes, pcs):
    count = pcs.shape[1]
    design = jnp.concatenate([jnp.ones((1, count), jnp.float32), pcs.astype(jnp.float32)], axis=0)
    observed = genotypes >= 0.0
    dosage = jnp.where(observed, genotypes, 0.0).astype(jnp.float32)
    design_gram = jnp.dot(design, design.T, precision=lax.Precision.HIGHEST)
    cross = jnp.dot(design, dosage.T, precision=lax.Precision.HIGHEST)
    factor = jnp.linalg.cholesky(design_gram)
    coef = jax.scipy.linalg.cho_solve((factor, True), cross)
    fitted = jnp.dot(coef.T, design, precision=lax.Precision.HIGHEST)
    freq = jnp.clip(0.5 * fitted, 0.02, 0.98)
    resid = jnp.where(observed, dosage - 2.0 * freq, 0.0).astype(jnp.bfloat16)
    spread = jnp.where(observed, jnp.sqrt(freq * (1.0 - freq)), 0.0).astype(jnp.bfloat16)
    numer = jnp.dot(resid.T.astype(jnp.float32), resid.astype(jnp.float32), preferred_element_type=jnp.float32)
    denom = jnp.dot(spread.T.astype(jnp.float32), spread.astype(jnp.float32), preferred_element_type=jnp.float32)
    return numer / (4.0 * denom)
```

```python
import jax
import jax.numpy as jnp
from jax import lax
from jax.sharding import PartitionSpec as P

HIGH = lax.Precision.HIGHEST
LINK = jnp.float16
OVER_ROWS = (((0,), (0,)), ((), ()))


def solve_coef(design, cross):
    gram = jnp.dot(design, design.T, precision=HIGH)
    factor = jnp.linalg.cholesky(gram)
    return jax.scipy.linalg.cho_solve((factor, True), cross)


def resid_spread(shifted, coef, design):
    observed = shifted >= -1.5
    fitted = lax.dot_general(coef, design, OVER_ROWS, precision=HIGH)
    freq = jnp.clip(0.5 * fitted, 0.02, 0.98)
    resid = jnp.where(observed, (shifted + 1.0) - 2.0 * freq, 0.0)
    spread = jnp.where(observed, jnp.sqrt(freq * (1.0 - freq)), 0.0)
    return resid.astype(jnp.bfloat16), spread.astype(jnp.bfloat16)


def pair_sums(left, right):
    numer = lax.dot_general(left[0], right[0], OVER_ROWS, preferred_element_type=jnp.float32)
    denom = lax.dot_general(left[1], right[1], OVER_ROWS, preferred_element_type=jnp.float32)
    return jnp.stack([numer, denom])


def pick(index, options):
    items = sorted(options.items())
    out = items[0][1]
    for value, array in items[1:]:
        if array is not out:
            out = jnp.where(index == value, array, out)
    return out


def make_body(snp_n, samp_n):
    both = ("snp", "samp")

    def flat(s, z):
        return s * samp_n + z

    def body(genotypes, pcs):
        width = genotypes.shape[1]
        half = width // 2
        s = lax.axis_index("snp")
        z = lax.axis_index("samp")
        core = lax.rem(s, 2)
        chip = lax.div(s, 2)

        coded = (genotypes - 1.0).astype(LINK)
        halves = [coded[:, :half], coded[:, half:]]
        right = {0: halves}
        left = {0: halves}
        for k in range(1, samp_n):
            up = [(i, i + 1) for i in range(k - 1, samp_n - 1)]
            down = [(samp_n - 1 - a, samp_n - 1 - b) for a, b in up]
            right[k], left[k] = [], []
            for h in range(2):
                right[k].append(lax.ppermute(right[k - 1][h], "samp", up))
                left[k].append(lax.ppermute(left[k - 1][h], "samp", down))

        design = jnp.concatenate([jnp.ones((1, width), jnp.float32), pcs], axis=0)
        dosage = jnp.where(genotypes >= 0.0, genotypes, 0.0)
        cross_part = lax.dot_general(design, dosage, (((1,), (1,)), ((), ())), precision=HIGH)
        mine = jnp.concatenate([cross_part, design], axis=1)
        theirs = [mine]
        for j in range(1, samp_n):
            theirs.append(lax.ppermute(mine, "samp", [(i, i ^ j) for i in range(samp_n)]))
        snps = cross_part.shape[1]
        cross = sum(t[:, :snps] for t in theirs)
        designs = [t[:, snps:] for t in theirs]
        coef = solve_coef(jnp.concatenate(designs, axis=1), cross)

        own = resid_spread(genotypes - 1.0, coef, design)

        units = []
        for j in range(samp_n):
            keep, give = None, None
            parts = []
            for h in range(2):
                if j == 0:
                    rows = (own[0][:, h * half:(h + 1) * half], own[1][:, h * half:(h + 1) * half])
                else:
                    options = {}
                    for i in range(samp_n):
                        b = i ^ j
                        options[i] = left[b - i][h] if b > i else right[i - b][h]
                    block = pick(z, options).astype(jnp.float32)
                    rows = resid_spread(block, coef, designs[j][:, h * half:(h + 1) * half])
                parts.append(pair_sums(rows, own))
            give = jnp.where(core == 0, parts[1], parts[0]).astype(LINK)
            keep = jnp.where(core == 0, parts[0], parts[1])
            got = lax.ppermute(give, "snp", [(i, i ^ 1) for i in range(snp_n)])
            units.append(keep + got.astype(jnp.float32))

        stacked = jnp.stack([u.astype(LINK) for u in units])
        last = samp_n - 1
        total = pick(chip ^ z, {j: units[j] for j in range(samp_n)})
        for d in range(1, samp_n):
            chosen = lax.dynamic_index_in_dim(stacked[:last], jnp.minimum(chip ^ z ^ d, last - 1), 0, keepdims=False)
            early, late = [], []
            for i in range(snp_n):
                for k in range(samp_n):
                    pair = (flat(i, k), flat(i ^ (2 * d), k))
                    (late if (i // 2) ^ k ^ d == last else early).append(pair)
            total = total + lax.ppermute(chosen, both, early).astype(jnp.float32)
            total = total + lax.ppermute(stacked[last], both, late).astype(jnp.float32)
        return total[0] / (4.0 * total[1])

    return body


def plain(genotypes, pcs):
    width = genotypes.shape[1]
    design = jnp.concatenate([jnp.ones((1, width), jnp.float32), pcs], axis=0)
    dosage = jnp.where(genotypes >= 0.0, genotypes, 0.0)
    cross_part = lax.dot_general(design, dosage, (((1,), (1,)), ((), ())), precision=HIGH)
    cross = lax.psum(cross_part, "samp")
    full = lax.all_gather(design, "samp", axis=1, tiled=True)
    coef = solve_coef(full, cross)
    own = resid_spread(genotypes - 1.0, coef, design)
    rows = lax.all_gather(jnp.stack(own), "samp", axis=2, tiled=True)
    sums = lax.psum_scatter(pair_sums(rows, own), "snp", scatter_dimension=1, tiled=True)
    return sums[0] / (4.0 * sums[1])


def solution(mesh):
    snp_n, samp_n = mesh.shape["snp"], mesh.shape["samp"]
    paired = snp_n == 2 * samp_n and samp_n & (samp_n - 1) == 0
    body = make_body(snp_n, samp_n) if paired else plain
    in_specs = (P("snp", "samp"), P(None, "samp"))
    return jax.shard_map(body, mesh=mesh, in_specs=in_specs, out_specs=P("snp", "samp"), check_vma=False)
```

```python
import functools

import jax
import jax.numpy as jnp
from jax import lax
from jax.experimental import pallas as pl
from jax.experimental.pallas import tpu as pltpu
from jax.sharding import PartitionSpec as P

HIGH = lax.Precision.HIGHEST
LINK = jnp.float16
OVER_ROWS = (((0,), (0,)), ((), ()))
RANGE = 120.0
PAD = 32
VMEM_BYTES = 56 * 2**20
DESIGN_ROWS = 21
STEP = 256
FREE = pl.CostEstimate(flops=0, bytes_accessed=0, transcendentals=0)


def solve_coef(design, cross):
    gram = jnp.dot(design, design.T, precision=HIGH)
    factor = jnp.linalg.cholesky(gram)
    return jax.scipy.linalg.cho_solve((factor, True), cross)


def encode(genotypes):
    return jnp.where(genotypes >= 0.0, jnp.exp2(RANGE * genotypes - RANGE), 0.0).astype(jnp.bfloat16)


def decode(coded):
    value = coded.astype(jnp.float32)
    observed = value > 0.0
    return jnp.log2(jnp.where(observed, value, 1.0)) * (1.0 / RANGE) + 1.0, observed


def thirds(x):
    a = x.astype(jnp.bfloat16)
    rest = x - a.astype(jnp.float32)
    b = rest.astype(jnp.bfloat16)
    return a, b, (rest - b.astype(jnp.float32)).astype(jnp.bfloat16)


def left_stack(x):
    a, b, c = thirds(x)
    return jnp.concatenate([a, a, b, b, a, c], axis=0)


def right_stack(y):
    a, b, c = thirds(y)
    return jnp.concatenate([a, b, a, b, c, a], axis=0)


def resid_spread(dosage, observed, fitted):
    twice = jnp.clip(fitted, 0.04, 1.96)
    product = twice * (2.0 - twice)
    resid = jnp.where(observed, dosage - twice, 0.0)
    spread = jnp.where(observed, 0.5 * jnp.sqrt(product), 0.0)
    return resid.astype(jnp.bfloat16), spread.astype(jnp.bfloat16)


def product(left, right):
    return lax.dot_general(left, right, OVER_ROWS, preferred_element_type=jnp.float32)


def coef_kernel(mine_ref, a_ref, b_ref, c_ref, coef_ref):
    rows, snps = mine_ref.shape[0], coef_ref.shape[1]
    across_lanes = (((1,), (1,)), ((), ()))
    cross = mine_ref[:, :snps] + a_ref[:, :snps] + b_ref[:, :snps] + c_ref[:, :snps]
    gram = jnp.zeros((rows, rows), jnp.float32)
    for ref in (mine_ref, a_ref, b_ref, c_ref):
        design = ref[:, snps:]
        gram = gram + lax.dot_general(design, design, across_lanes, precision=HIGH, preferred_element_type=jnp.float32)
    row = lax.broadcasted_iota(jnp.int32, (rows, rows), 0)
    unit = (row == lax.broadcasted_iota(jnp.int32, (rows, rows), 1)).astype(jnp.float32)
    gram = gram + jnp.where(row >= DESIGN_ROWS, unit, 0.0)
    left, inverse = gram, unit
    for j in range(DESIGN_ROWS):
        pivot = 1.0 / left[j:j + 1, j:j + 1]
        factor = (left[:, j:j + 1] - unit[:, j:j + 1]) * pivot
        left, inverse = left - factor * left[j:j + 1, :], inverse - factor * inverse[j:j + 1, :]
    coef = jnp.dot(inverse, cross, precision=HIGH, preferred_element_type=jnp.float32)
    rest = cross - jnp.dot(gram, coef, precision=HIGH, preferred_element_type=jnp.float32)
    coef = coef + jnp.dot(inverse, rest, precision=HIGH, preferred_element_type=jnp.float32)
    coef_ref[...] = jnp.concatenate([coef, jnp.zeros((PAD - rows, snps), jnp.float32)], axis=0)


def coefficients(theirs, snps):
    vmem = pl.BlockSpec(memory_space=pltpu.VMEM)
    return pl.pallas_call(
        coef_kernel,
        out_shape=jax.ShapeDtypeStruct((PAD, snps), jnp.float32),
        in_specs=[vmem] * 4,
        out_specs=vmem,
        compiler_params=pltpu.CompilerParams(vmem_limit_bytes=VMEM_BYTES),
        cost_estimate=FREE,
    )(*theirs)


def own_kernel(core_ref, own_ref, coef_ref, design_ref, terms_ref, sums_ref, coefs, designs):
    _, _, _, quarter, width = sums_ref.shape
    snps = coef_ref.shape[1]
    coefs[...] = left_stack(coef_ref[...])
    designs[...] = right_stack(design_ref[...])

    def terms(k, _):
        at = pl.ds(pl.multiple_of(k * STEP, STEP), STEP)
        dosage = own_ref[at, :]
        fitted = product(coefs[:, at], designs[...])
        terms_ref[0, at, :], terms_ref[1, at, :] = resid_spread(dosage, dosage >= 0.0, fitted)
        return 0

    lax.fori_loop(0, snps // STEP, terms, 0)
    for p in range(2):
        for h in range(2):
            first = (2 * h + p) * quarter
            for t in range(2):
                sums_ref[jnp.bitwise_xor(core_ref[0], h), p, t] = product(terms_ref[t, :, first:first + quarter], terms_ref[t])


def block_kernel(sources, place_ref, terms_ref, coef_ref, design_ref, *refs):
    *coded, sums_ref, coefs, designs, rows_ref = refs
    _, _, _, quarter, width = sums_ref.shape
    snps = coef_ref.shape[1]
    coefs[...] = left_stack(coef_ref[...])
    designs[...] = right_stack(design_ref[...])

    def terms(k, _):
        at = pl.ds(pl.multiple_of(k * STEP, STEP), STEP)
        fitted = product(coefs[:, at], designs[...])
        for g, choices in enumerate(sources):
            here = slice(2 * g * quarter, 2 * (g + 1) * quarter)
            values = [coded[i][at, first:first + 2 * quarter] for i, first in choices]
            value = values[0] if len(values) == 1 else jnp.where(place_ref[1] == 1, values[0], values[1])
            dosage, observed = decode(value)
            rows_ref[0, at, here], rows_ref[1, at, here] = resid_spread(dosage, observed, fitted[:, here])
        return 0

    lax.fori_loop(0, snps // STEP, terms, 0)
    for g in range(2):
        for h in range(2):
            first = (2 * g + h) * quarter
            for t in range(2):
                sums_ref[jnp.bitwise_xor(place_ref[0], h), g, t] = product(rows_ref[t, :, first:first + quarter], terms_ref[t])


def block_sums(place, coef, design, own=None, terms=None, coded=(), sources=None):
    snps, width = coef.shape[1], design.shape[1]
    vmem = pl.BlockSpec(memory_space=pltpu.VMEM)
    pair = (2, snps, width)
    sums = jax.ShapeDtypeStruct((2, 2, 2, width // 4, width), jnp.float32)
    scratch = [pltpu.VMEM((6 * PAD, snps), jnp.bfloat16), pltpu.VMEM((6 * PAD, width), jnp.bfloat16)]
    if own is not None:
        kernel, operands = own_kernel, (place, own, coef, design)
        out = (jax.ShapeDtypeStruct(pair, jnp.bfloat16), sums)
    else:
        kernel, operands = functools.partial(block_kernel, sources), (place, terms, coef, design, *coded)
        out = sums
        scratch.append(pltpu.VMEM(pair, jnp.bfloat16))
    return pl.pallas_call(
        kernel,
        out_shape=out,
        in_specs=[pl.BlockSpec(memory_space=pltpu.SMEM)] + [vmem] * (len(operands) - 1),
        out_specs=jax.tree.map(lambda _: vmem, out),
        scratch_shapes=scratch,
        compiler_params=pltpu.CompilerParams(vmem_limit_bytes=VMEM_BYTES),
        cost_estimate=FREE,
    )(*operands)


def kinship(sums):
    return sums[0] / (4.0 * sums[1])


def after(value, *earlier):
    return lax.optimization_barrier((value, *earlier))[0]


def padded(x):
    return jnp.pad(x, ((0, PAD - x.shape[0]), (0, 0)))


def line_of_four(genotypes, pcs):
    both = ("snp", "samp")
    width = genotypes.shape[1]
    half, quarter = width // 2, width // 4
    s = lax.axis_index("snp")
    z = lax.axis_index("samp")
    core = lax.rem(s, 2)
    chip = lax.div(s, 2)
    inner = jnp.logical_or(z == 1, z == 2).astype(jnp.int32)
    place = jnp.stack([core, inner])
    other_core = [(i, i ^ 1) for i in range(8)]

    def by_parts(array):
        return jnp.concatenate([array[:, i * quarter:(i + 1) * quarter] for i in (0, 2, 1, 3)], axis=1)

    def part(array, p):
        return array[:, p * half:(p + 1) * half]

    swap = [(0, 1), (1, 0), (2, 3), (3, 2)]
    middle = [(1, 2), (2, 1)]
    outward = [(1, 0), (2, 3)]
    ends = [(0, 3), (3, 0)]
    coded = encode(by_parts(genotypes))
    near = lax.ppermute(coded, "samp", swap)
    across = lax.ppermute(coded, "samp", middle)
    far = [lax.ppermute(part(near, p), "samp", middle) for p in range(2)]
    out = [lax.ppermute(part(across, p), "samp", outward) for p in range(2)]
    direct = after(coded, near, across)
    end = [lax.ppermute(part(direct, p), "samp", ends) for p in range(2)]

    design = jnp.concatenate([jnp.ones((1, width), jnp.float32), pcs], axis=0)
    design = jnp.pad(design, ((0, -DESIGN_ROWS % 8), (0, 0)))
    dosage = jnp.where(genotypes >= 0.0, genotypes, 0.0)
    cross_part = lax.dot_general(design, dosage, (((1,), (1,)), ((), ())), precision=HIGH)
    snps = cross_part.shape[1]
    mine = jnp.concatenate([cross_part, design], axis=1)
    theirs = [mine] + [lax.ppermute(mine, "samp", [(i, i ^ j) for i in range(4)]) for j in range(1, 4)]
    theirs = [after(t, near, across) for t in theirs]
    coef = coefficients(theirs, snps)
    designs = [padded(t[:, snps:]) for t in theirs]

    terms, own = block_sums(place, coef, designs[0], own=genotypes)
    first = block_sums(place, coef, by_parts(designs[1]), terms=terms, coded=(near,), sources=(((0, 0),), ((0, half),)))
    two, three = by_parts(designs[2]), by_parts(designs[3])
    rows = []
    for p in range(2):
        late = block_sums(
            place,
            coef,
            jnp.concatenate([part(two, p), part(three, p)], axis=1),
            terms=terms,
            coded=(far[p], out[p], across, end[p]),
            sources=(((0, 0), (1, 0)), ((2, p * half), (3, 0))),
        )

        def units(side):
            return jnp.concatenate([own[side, p:p + 1], first[side, p:p + 1], late[side]])

        got = lax.ppermute(units(1).astype(LINK), "snp", other_core)
        sums = units(0) + got.astype(jnp.float32)
        total = lax.dynamic_index_in_dim(sums, chip ^ z, 0, keepdims=False)
        for d in range(1, 4):
            chosen = lax.dynamic_index_in_dim(sums, chip ^ z ^ d, 0, keepdims=False).astype(LINK)
            total = total + lax.ppermute(chosen, "snp", [(i, i ^ (2 * d)) for i in range(8)]).astype(jnp.float32)
        rows.append(kinship(total))
    return jnp.concatenate(rows, axis=0)


def any_mesh(genotypes, pcs):
    width = genotypes.shape[1]
    design = jnp.concatenate([jnp.ones((1, width), jnp.float32), pcs], axis=0)
    observed = genotypes >= 0.0
    dosage = jnp.where(observed, genotypes, 0.0)
    cross_part = lax.dot_general(design, dosage, (((1,), (1,)), ((), ())), precision=HIGH)
    cross = lax.psum(cross_part, "samp")
    full = lax.all_gather(design, "samp", axis=1, tiled=True)
    fitted = lax.dot_general(solve_coef(full, cross), design, OVER_ROWS, precision=HIGH)
    own = resid_spread(dosage, observed, fitted)
    rows = lax.all_gather(jnp.stack(own), "samp", axis=2, tiled=True)
    sums = jnp.stack([product(rows[t], own[t]) for t in range(2)])
    return kinship(lax.psum_scatter(sums, "snp", scatter_dimension=1, tiled=True))


def solution(mesh):
    body = line_of_four if (mesh.shape["snp"], mesh.shape["samp"]) == (8, 4) else any_mesh
    in_specs = (P("snp", "samp"), P(None, "samp"))
    return jax.shard_map(body, mesh=mesh, in_specs=in_specs, out_specs=P("snp", "samp"), check_vma=False)
```

```python
import functools

import jax
import jax.numpy as jnp
from jax import lax
from jax.experimental import pallas as pl
from jax.experimental.pallas import tpu as pltpu
from jax.sharding import PartitionSpec as P

HIGH = lax.Precision.HIGHEST
LINK = jnp.float16
OVER_ROWS = (((0,), (0,)), ((), ()))
RANGE = 120.0
PAD = 32
VMEM_BYTES = 24 * 2**20
DESIGN_ROWS = 21
STEP = 256
FREE = pl.CostEstimate(flops=0, bytes_accessed=0, transcendentals=0)


def solve_coef(design, cross):
    gram = jnp.dot(design, design.T, precision=HIGH)
    factor = jnp.linalg.cholesky(gram)
    return jax.scipy.linalg.cho_solve((factor, True), cross)


def encode(genotypes):
    return jnp.where(genotypes >= 0.0, jnp.exp2(RANGE * genotypes - RANGE), 0.0).astype(jnp.bfloat16)


def decode(coded):
    value = coded.astype(jnp.float32)
    observed = value > 0.0
    return jnp.log2(jnp.where(observed, value, 1.0)) * (1.0 / RANGE) + 1.0, observed


def thirds(x):
    a = x.astype(jnp.bfloat16)
    rest = x - a.astype(jnp.float32)
    b = rest.astype(jnp.bfloat16)
    return a, b, (rest - b.astype(jnp.float32)).astype(jnp.bfloat16)


def left_stack(x):
    a, b, c = thirds(x)
    return jnp.concatenate([a, a, b, b, a, c], axis=0)


def right_stack(y):
    a, b, c = thirds(y)
    return jnp.concatenate([a, b, a, b, c, a], axis=0)


def resid_spread(dosage, observed, fitted):
    twice = jnp.clip(fitted, 0.04, 1.96)
    product = twice * (2.0 - twice)
    resid = jnp.where(observed, dosage - twice, 0.0)
    spread = jnp.where(observed, 0.5 * jnp.sqrt(product), 0.0)
    return resid.astype(jnp.bfloat16), spread.astype(jnp.bfloat16)


def product(left, right):
    return lax.dot_general(left, right, OVER_ROWS, preferred_element_type=jnp.float32)


def coef_kernel(mine_ref, a_ref, b_ref, c_ref, coef_ref):
    rows, snps = mine_ref.shape[0], coef_ref.shape[1]
    across_lanes = (((1,), (1,)), ((), ()))
    cross = mine_ref[:, :snps] + a_ref[:, :snps] + b_ref[:, :snps] + c_ref[:, :snps]
    gram = jnp.zeros((rows, rows), jnp.float32)
    for ref in (mine_ref, a_ref, b_ref, c_ref):
        design = ref[:, snps:]
        gram = gram + lax.dot_general(design, design, across_lanes, precision=HIGH, preferred_element_type=jnp.float32)
    row = lax.broadcasted_iota(jnp.int32, (rows, rows), 0)
    unit = (row == lax.broadcasted_iota(jnp.int32, (rows, rows), 1)).astype(jnp.float32)
    gram = gram + jnp.where(row >= DESIGN_ROWS, unit, 0.0)
    left, inverse = gram, unit
    for j in range(DESIGN_ROWS):
        pivot = 1.0 / left[j:j + 1, j:j + 1]
        factor = (left[:, j:j + 1] - unit[:, j:j + 1]) * pivot
        left, inverse = left - factor * left[j:j + 1, :], inverse - factor * inverse[j:j + 1, :]
    coef = jnp.dot(inverse, cross, precision=HIGH, preferred_element_type=jnp.float32)
    rest = cross - jnp.dot(gram, coef, precision=HIGH, preferred_element_type=jnp.float32)
    coef = coef + jnp.dot(inverse, rest, precision=HIGH, preferred_element_type=jnp.float32)
    coef_ref[...] = jnp.concatenate([coef, jnp.zeros((PAD - rows, snps), jnp.float32)], axis=0)


def coefficients(theirs, snps):
    vmem = pl.BlockSpec(memory_space=pltpu.VMEM)
    return pl.pallas_call(
        coef_kernel,
        out_shape=jax.ShapeDtypeStruct((PAD, snps), jnp.float32),
        in_specs=[vmem] * 4,
        out_specs=vmem,
        compiler_params=pltpu.CompilerParams(vmem_limit_bytes=VMEM_BYTES),
        cost_estimate=FREE,
    )(*theirs)


def pack(sums):
    size = jnp.exp2(8.0 * jnp.log2(jnp.maximum(jnp.abs(sums), 1e-30)) + 20.0)
    return jnp.where(sums < 0.0, -size, size).astype(jnp.bfloat16)


def unpack(packed):
    value = packed.astype(jnp.float32)
    size = jnp.abs(value)
    sums = jnp.exp2(jnp.log2(jnp.where(size > 0.0, size, 1.0)) * 0.125 - 2.5)
    return jnp.where(size > 0.0, jnp.where(value < 0.0, -sums, sums), 0.0)


def split_cores(first_core, left, right, keep_ref, give_ref, g, order):
    quarter = keep_ref.shape[2]
    for t in range(2):
        a, b = [product(left[t, :, first:first + quarter], right[t]) for first in order]
        keep_ref[g, t] = jnp.where(first_core, a, b)
        give_ref[g, t] = pack(jnp.where(first_core, b, a))


def own_kernel(place_ref, own_ref, coef_ref, design_ref, terms_ref, keep_ref, give_ref, coefs, designs):
    quarter = keep_ref.shape[2]
    snps = coef_ref.shape[1]
    coefs[...] = left_stack(coef_ref[...])
    designs[...] = right_stack(design_ref[...])

    def terms(k, _):
        at = pl.ds(pl.multiple_of(k * STEP, STEP), STEP)
        dosage = own_ref[at, :]
        fitted = product(coefs[:, at], designs[...])
        terms_ref[0, at, :], terms_ref[1, at, :] = resid_spread(dosage, dosage >= 0.0, fitted)
        return 0

    lax.fori_loop(0, snps // STEP, terms, 0)
    for p in range(2):
        split_cores(place_ref[0] == 0, terms_ref, terms_ref, keep_ref, give_ref, p, (p * quarter, (2 + p) * quarter))


def block_kernel(sources, place_ref, terms_ref, coef_ref, design_ref, *refs):
    *coded, keep_ref, give_ref, coefs, designs, rows_ref = refs
    quarter = keep_ref.shape[2]
    snps = coef_ref.shape[1]
    coefs[...] = left_stack(coef_ref[...])
    designs[...] = right_stack(design_ref[...])

    def terms(k, _):
        at = pl.ds(pl.multiple_of(k * STEP, STEP), STEP)
        fitted = product(coefs[:, at], designs[...])
        for g, choices in enumerate(sources):
            here = slice(2 * g * quarter, 2 * (g + 1) * quarter)
            values = [coded[i][at, :] for i in choices]
            value = values[0] if len(values) == 1 else jnp.where(place_ref[1] == 1, values[0], values[1])
            dosage, observed = decode(value)
            rows_ref[0, at, here], rows_ref[1, at, here] = resid_spread(dosage, observed, fitted[:, here])
        return 0

    lax.fori_loop(0, snps // STEP, terms, 0)
    for g in range(2):
        split_cores(place_ref[0] == 0, rows_ref, terms_ref, keep_ref, give_ref, g, (2 * g * quarter, (2 * g + 1) * quarter))


def block_sums(place, coef, design, own=None, terms=None, coded=(), sources=None):
    snps, width = coef.shape[1], design.shape[1]
    vmem = pl.BlockSpec(memory_space=pltpu.VMEM)
    pair = (2, snps, width)
    sums = (2, 2, width // 4, width)
    out = (jax.ShapeDtypeStruct(sums, jnp.float32), jax.ShapeDtypeStruct(sums, jnp.bfloat16))
    scratch = [pltpu.VMEM((6 * PAD, snps), jnp.bfloat16), pltpu.VMEM((6 * PAD, width), jnp.bfloat16)]
    if own is not None:
        kernel, operands = own_kernel, (place, own, coef, design)
        out = (jax.ShapeDtypeStruct(pair, jnp.bfloat16),) + out
    else:
        kernel, operands = functools.partial(block_kernel, sources), (place, terms, coef, design, *coded)
        scratch.append(pltpu.VMEM(pair, jnp.bfloat16))
    return pl.pallas_call(
        kernel,
        out_shape=out,
        in_specs=[pl.BlockSpec(memory_space=pltpu.SMEM)] + [vmem] * (len(operands) - 1),
        out_specs=tuple(vmem for _ in out),
        scratch_shapes=scratch,
        compiler_params=pltpu.CompilerParams(vmem_limit_bytes=VMEM_BYTES),
        cost_estimate=FREE,
    )(*operands)


def add_kernel(place_ref, own_ref, near_ref, late_ref, got_own_ref, got_near_ref, got_late_ref, mine_ref, *refs):
    *sent, sums = refs
    pairs = ((own_ref, 0, got_own_ref), (near_ref, 0, got_near_ref), (late_ref, 0, got_late_ref), (late_ref, 1, got_late_ref))
    for j, (kept, i, got) in enumerate(pairs):
        sums[j] = kept[i] + unpack(got[i])
    mine_ref[...] = sums[place_ref[2]]
    for d, ref in enumerate(sent, 1):
        ref[...] = pack(sums[jnp.bitwise_xor(place_ref[2], d)])


def add_cores(place, p, own, near, late, got_own, got_near, got_late):
    shape = late.shape[1:]
    one = pl.BlockSpec((1,) + shape, lambda i: (p, 0, 0, 0))
    both = pl.BlockSpec((2,) + shape, lambda i: (0, 0, 0, 0))
    whole = pl.BlockSpec(shape, lambda i: (0, 0, 0))
    return pl.pallas_call(
        add_kernel,
        grid=(1,),
        out_shape=(jax.ShapeDtypeStruct(shape, jnp.float32),) + (jax.ShapeDtypeStruct(shape, jnp.bfloat16),) * 3,
        in_specs=[pl.BlockSpec(memory_space=pltpu.SMEM), one, one, both, one, one, both],
        out_specs=(whole,) * 4,
        scratch_shapes=[pltpu.VMEM((4,) + shape, jnp.float32)],
        compiler_params=pltpu.CompilerParams(vmem_limit_bytes=VMEM_BYTES),
        cost_estimate=FREE,
    )(place, own, near, late, got_own, got_near, got_late)


def divide_kernel(*refs):
    *parts, out_ref = refs
    quarter = out_ref.shape[0] // 2
    for p in range(2):
        mine, *got = parts[4 * p:4 * p + 4]
        sums = [mine[t] + unpack(got[0][t]) + unpack(got[1][t]) + unpack(got[2][t]) for t in range(2)]
        out_ref[p * quarter:(p + 1) * quarter, :] = sums[0] / (4.0 * sums[1])


def divide(parts):
    _, quarter, width = parts[0].shape
    vmem = pl.BlockSpec(memory_space=pltpu.VMEM)
    return pl.pallas_call(
        divide_kernel,
        out_shape=jax.ShapeDtypeStruct((2 * quarter, width), jnp.float32),
        in_specs=[vmem] * len(parts),
        out_specs=vmem,
        compiler_params=pltpu.CompilerParams(vmem_limit_bytes=VMEM_BYTES),
        cost_estimate=FREE,
    )(*parts)


def kinship(sums):
    return sums[0] / (4.0 * sums[1])


def after(value, *earlier):
    return lax.optimization_barrier((value, *earlier))[0]


def padded(x):
    return jnp.pad(x, ((0, PAD - x.shape[0]), (0, 0)))


def line_of_four(genotypes, pcs):
    width = genotypes.shape[1]
    half, quarter = width // 2, width // 4
    s = lax.axis_index("snp")
    z = lax.axis_index("samp")
    chip = lax.div(s, 2)
    place = jnp.stack([lax.rem(s, 2), jnp.logical_or(z == 1, z == 2).astype(jnp.int32), chip ^ z])
    other_core = [(i, i ^ 1) for i in range(8)]

    def part(array, p):
        a, b = p * quarter, p * quarter + half
        return jnp.concatenate([array[:, a:a + quarter], array[:, b:b + quarter]], axis=1)

    coded = [encode(part(genotypes, p)) for p in range(2)]
    near = [lax.ppermute(c, "samp", [(i, i ^ 1) for i in range(4)]) for c in coded]
    three = [lax.ppermute(c, "samp", [(i, i ^ 3) for i in range(4)]) for c in coded]
    far = [lax.ppermute(c, "samp", [(1, 2), (2, 1)]) for c in near]
    out = [lax.ppermute(c, "samp", [(1, 0), (2, 3)]) for c in three]

    design = jnp.concatenate([jnp.ones((1, width), jnp.float32), pcs], axis=0)
    design = jnp.pad(design, ((0, -DESIGN_ROWS % 8), (0, 0)))
    dosage = jnp.where(genotypes >= 0.0, genotypes, 0.0)
    cross_part = lax.dot_general(design, dosage, (((1,), (1,)), ((), ())), precision=HIGH)
    snps = cross_part.shape[1]
    mine = jnp.concatenate([cross_part, design], axis=1)
    theirs = [mine] + [lax.ppermute(mine, "samp", [(i, i ^ j) for i in range(4)]) for j in range(1, 4)]
    coef = coefficients(theirs, snps)
    designs = [padded(t[:, snps:]) for t in theirs]

    terms, keep_own, give_own = block_sums(place, coef, designs[0], own=genotypes)
    near_design = jnp.concatenate([part(designs[1], 0), part(designs[1], 1)], axis=1)
    keep_near, give_near = block_sums(place, coef, near_design, terms=terms, coded=near, sources=((0,), (1,)))
    got_own, got_near = [lax.ppermute(g, "snp", other_core) for g in (give_own, give_near)]
    parts = []
    for p in range(2):
        late_design = jnp.concatenate([part(designs[2], p), part(designs[3], p)], axis=1)
        keep, give = block_sums(place, coef, late_design, terms=terms, coded=(far[p], out[p], three[p]), sources=((0, 1), (2,)))
        got = lax.ppermute(give, "snp", other_core)
        mine, *sent = add_cores(place, p, keep_own, keep_near, keep, got_own, got_near, got)
        parts.append(mine)
        for d in range(1, 4):
            parts.append(lax.ppermute(sent[d - 1], "snp", [(i, i ^ (2 * d)) for i in range(8)]))
    return divide(parts)


def any_mesh(genotypes, pcs):
    width = genotypes.shape[1]
    design = jnp.concatenate([jnp.ones((1, width), jnp.float32), pcs], axis=0)
    observed = genotypes >= 0.0
    dosage = jnp.where(observed, genotypes, 0.0)
    cross_part = lax.dot_general(design, dosage, (((1,), (1,)), ((), ())), precision=HIGH)
    cross = lax.psum(cross_part, "samp")
    full = lax.all_gather(design, "samp", axis=1, tiled=True)
    fitted = lax.dot_general(solve_coef(full, cross), design, OVER_ROWS, precision=HIGH)
    own = resid_spread(dosage, observed, fitted)
    rows = lax.all_gather(jnp.stack(own), "samp", axis=2, tiled=True)
    sums = jnp.stack([product(rows[t], own[t]) for t in range(2)])
    return kinship(lax.psum_scatter(sums, "snp", scatter_dimension=1, tiled=True))


def solution(mesh):
    body = line_of_four if (mesh.shape["snp"], mesh.shape["samp"]) == (8, 4) else any_mesh
    in_specs = (P("snp", "samp"), P(None, "samp"))
    return jax.shard_map(body, mesh=mesh, in_specs=in_specs, out_specs=P("snp", "samp"), check_vma=False)
```

```python
import functools

import jax
import jax.numpy as jnp
from jax import lax
from jax.experimental import pallas as pl
from jax.experimental.pallas import tpu as pltpu
from jax.sharding import PartitionSpec as P

HIGH = lax.Precision.HIGHEST
LINK = jnp.float16
OVER_ROWS = (((0,), (0,)), ((), ()))
RANGE = 120.0
PAD = 32
VMEM_BYTES = 24 * 2**20
DESIGN_ROWS = 21
STEP = 256
FREE = pl.CostEstimate(flops=0, bytes_accessed=0, transcendentals=0)


def solve_coef(design, cross):
    gram = jnp.dot(design, design.T, precision=HIGH)
    factor = jnp.linalg.cholesky(gram)
    return jax.scipy.linalg.cho_solve((factor, True), cross)


def encode(genotypes):
    return jnp.where(genotypes >= 0.0, jnp.exp2(RANGE * genotypes - RANGE), 0.0).astype(jnp.bfloat16)


def decode(coded):
    value = coded.astype(jnp.float32)
    observed = value > 0.0
    return jnp.log2(jnp.where(observed, value, 1.0)) * (1.0 / RANGE) + 1.0, observed


def thirds(x):
    a = x.astype(jnp.bfloat16)
    rest = x - a.astype(jnp.float32)
    b = rest.astype(jnp.bfloat16)
    return a, b, (rest - b.astype(jnp.float32)).astype(jnp.bfloat16)


def left_stack(x):
    a, b, c = thirds(x)
    return jnp.concatenate([a, a, b, b, a, c], axis=0)


def right_stack(y):
    a, b, c = thirds(y)
    return jnp.concatenate([a, b, a, b, c, a], axis=0)


def resid_spread(dosage, observed, fitted):
    twice = jnp.clip(fitted, 0.04, 1.96)
    product = twice * (2.0 - twice)
    resid = jnp.where(observed, dosage - twice, 0.0)
    spread = jnp.where(observed, 0.5 * jnp.sqrt(product), 0.0)
    return resid.astype(jnp.bfloat16), spread.astype(jnp.bfloat16)


def product(left, right):
    return lax.dot_general(left, right, OVER_ROWS, preferred_element_type=jnp.float32)


def coef_kernel(mine_ref, a_ref, b_ref, c_ref, coef_ref):
    rows, snps = mine_ref.shape[0], coef_ref.shape[1]
    across_lanes = (((1,), (1,)), ((), ()))
    cross = mine_ref[:, :snps] + a_ref[:, :snps] + b_ref[:, :snps] + c_ref[:, :snps]
    gram = jnp.zeros((rows, rows), jnp.float32)
    for ref in (mine_ref, a_ref, b_ref, c_ref):
        design = ref[:, snps:]
        gram = gram + lax.dot_general(design, design, across_lanes, precision=HIGH, preferred_element_type=jnp.float32)
    row = lax.broadcasted_iota(jnp.int32, (rows, rows), 0)
    unit = (row == lax.broadcasted_iota(jnp.int32, (rows, rows), 1)).astype(jnp.float32)
    gram = gram + jnp.where(row >= DESIGN_ROWS, unit, 0.0)
    left, inverse = gram, unit
    for j in range(DESIGN_ROWS):
        pivot = 1.0 / left[j:j + 1, j:j + 1]
        factor = (left[:, j:j + 1] - unit[:, j:j + 1]) * pivot
        left, inverse = left - factor * left[j:j + 1, :], inverse - factor * inverse[j:j + 1, :]
    coef = jnp.dot(inverse, cross, precision=HIGH, preferred_element_type=jnp.float32)
    rest = cross - jnp.dot(gram, coef, precision=HIGH, preferred_element_type=jnp.float32)
    coef = coef + jnp.dot(inverse, rest, precision=HIGH, preferred_element_type=jnp.float32)
    coef_ref[...] = jnp.concatenate([coef, jnp.zeros((PAD - rows, snps), jnp.float32)], axis=0)


def coefficients(theirs, snps):
    vmem = pl.BlockSpec(memory_space=pltpu.VMEM)
    return pl.pallas_call(
        coef_kernel,
        out_shape=jax.ShapeDtypeStruct((PAD, snps), jnp.float32),
        in_specs=[vmem] * 4,
        out_specs=vmem,
        compiler_params=pltpu.CompilerParams(vmem_limit_bytes=VMEM_BYTES),
        cost_estimate=pl.CostEstimate(flops=2 * 10**10, bytes_accessed=0, transcendentals=0),
    )(*theirs)


def pack(sums):
    size = jnp.exp2(8.0 * jnp.log2(jnp.maximum(jnp.abs(sums), 1e-30)) + 20.0)
    return jnp.where(sums < 0.0, -size, size).astype(jnp.bfloat16)


def unpack(packed):
    value = packed.astype(jnp.float32)
    size = jnp.abs(value)
    sums = jnp.exp2(jnp.log2(jnp.where(size > 0.0, size, 1.0)) * 0.125 - 2.5)
    return jnp.where(size > 0.0, jnp.where(value < 0.0, -sums, sums), 0.0)


def split_cores(first_core, left, right, keep_ref, give_ref, g, order):
    quarter = keep_ref.shape[2]
    for t in range(2):
        a, b = [product(left[t, :, first:first + quarter], right[t]) for first in order]
        keep_ref[g, t] = jnp.where(first_core, a, b)
        give_ref[g, t] = pack(jnp.where(first_core, b, a))


def own_kernel(place_ref, own_ref, coef_ref, design_ref, terms_ref, keep_ref, give_ref, coefs, designs):
    quarter = keep_ref.shape[2]
    snps = coef_ref.shape[1]
    coefs[...] = left_stack(coef_ref[...])
    designs[...] = right_stack(design_ref[...])

    def terms(k, _):
        at = pl.ds(pl.multiple_of(k * STEP, STEP), STEP)
        dosage = own_ref[at, :]
        fitted = product(coefs[:, at], designs[...])
        terms_ref[0, at, :], terms_ref[1, at, :] = resid_spread(dosage, dosage >= 0.0, fitted)
        return 0

    lax.fori_loop(0, snps // STEP, terms, 0)
    for p in range(2):
        split_cores(place_ref[0] == 0, terms_ref, terms_ref, keep_ref, give_ref, p, (p * quarter, (2 + p) * quarter))


def block_kernel(sources, place_ref, terms_ref, coef_ref, design_ref, *refs):
    *coded, keep_ref, give_ref, coefs, designs, rows_ref = refs
    quarter = keep_ref.shape[2]
    snps = coef_ref.shape[1]
    coefs[...] = left_stack(coef_ref[...])
    designs[...] = right_stack(design_ref[...])

    def terms(k, _):
        at = pl.ds(pl.multiple_of(k * STEP, STEP), STEP)
        fitted = product(coefs[:, at], designs[...])
        for g, choices in enumerate(sources):
            here = slice(2 * g * quarter, 2 * (g + 1) * quarter)
            values = [coded[i][at, :] for i in choices]
            value = values[0] if len(values) == 1 else jnp.where(place_ref[1] == 1, values[0], values[1])
            dosage, observed = decode(value)
            rows_ref[0, at, here], rows_ref[1, at, here] = resid_spread(dosage, observed, fitted[:, here])
        return 0

    lax.fori_loop(0, snps // STEP, terms, 0)
    for g in range(2):
        split_cores(place_ref[0] == 0, rows_ref, terms_ref, keep_ref, give_ref, g, (2 * g * quarter, (2 * g + 1) * quarter))


def block_sums(place, coef, design, own=None, terms=None, coded=(), sources=None):
    snps, width = coef.shape[1], design.shape[1]
    vmem = pl.BlockSpec(memory_space=pltpu.VMEM)
    pair = (2, snps, width)
    sums = (2, 2, width // 4, width)
    out = (jax.ShapeDtypeStruct(sums, jnp.float32), jax.ShapeDtypeStruct(sums, jnp.bfloat16))
    scratch = [pltpu.VMEM((6 * PAD, snps), jnp.bfloat16), pltpu.VMEM((6 * PAD, width), jnp.bfloat16)]
    if own is not None:
        kernel, operands = own_kernel, (place, own, coef, design)
        out = (jax.ShapeDtypeStruct(pair, jnp.bfloat16),) + out
    else:
        kernel, operands = functools.partial(block_kernel, sources), (place, terms, coef, design, *coded)
        scratch.append(pltpu.VMEM(pair, jnp.bfloat16))
    return pl.pallas_call(
        kernel,
        out_shape=out,
        in_specs=[pl.BlockSpec(memory_space=pltpu.SMEM)] + [vmem] * (len(operands) - 1),
        out_specs=tuple(vmem for _ in out),
        scratch_shapes=scratch,
        compiler_params=pltpu.CompilerParams(vmem_limit_bytes=VMEM_BYTES),
        cost_estimate=FREE,
    )(*operands)


def add_kernel(place_ref, own_ref, near_ref, late_ref, got_own_ref, got_near_ref, got_late_ref, mine_ref, *refs):
    *sent, sums = refs
    pairs = ((own_ref, 0, got_own_ref), (near_ref, 0, got_near_ref), (late_ref, 0, got_late_ref), (late_ref, 1, got_late_ref))
    for j, (kept, i, got) in enumerate(pairs):
        sums[j] = kept[i] + unpack(got[i])
    mine_ref[...] = sums[place_ref[2]]
    for d, ref in enumerate(sent, 1):
        ref[...] = pack(sums[jnp.bitwise_xor(place_ref[2], d)])


def add_cores(place, p, own, near, late, got_own, got_near, got_late):
    shape = late.shape[1:]
    one = pl.BlockSpec((1,) + shape, lambda i: (p, 0, 0, 0))
    both = pl.BlockSpec((2,) + shape, lambda i: (0, 0, 0, 0))
    whole = pl.BlockSpec(shape, lambda i: (0, 0, 0))
    return pl.pallas_call(
        add_kernel,
        grid=(1,),
        out_shape=(jax.ShapeDtypeStruct(shape, jnp.float32),) + (jax.ShapeDtypeStruct(shape, jnp.bfloat16),) * 3,
        in_specs=[pl.BlockSpec(memory_space=pltpu.SMEM), one, one, both, one, one, both],
        out_specs=(whole,) * 4,
        scratch_shapes=[pltpu.VMEM((4,) + shape, jnp.float32)],
        compiler_params=pltpu.CompilerParams(vmem_limit_bytes=VMEM_BYTES),
        cost_estimate=FREE,
    )(place, own, near, late, got_own, got_near, got_late)


def divide_kernel(*refs):
    *parts, out_ref = refs
    quarter = out_ref.shape[0] // 2
    for p in range(2):
        mine, *got = parts[4 * p:4 * p + 4]
        sums = [mine[t] + unpack(got[0][t]) + unpack(got[1][t]) + unpack(got[2][t]) for t in range(2)]
        out_ref[p * quarter:(p + 1) * quarter, :] = sums[0] / (4.0 * sums[1])


def divide(parts):
    _, quarter, width = parts[0].shape
    vmem = pl.BlockSpec(memory_space=pltpu.VMEM)
    return pl.pallas_call(
        divide_kernel,
        out_shape=jax.ShapeDtypeStruct((2 * quarter, width), jnp.float32),
        in_specs=[vmem] * len(parts),
        out_specs=vmem,
        compiler_params=pltpu.CompilerParams(vmem_limit_bytes=VMEM_BYTES),
        cost_estimate=FREE,
    )(*parts)


def kinship(sums):
    return sums[0] / (4.0 * sums[1])


def after(value, *earlier):
    return lax.optimization_barrier((value, *earlier))[0]


def padded(x):
    return jnp.pad(x, ((0, PAD - x.shape[0]), (0, 0)))


def line_of_four(genotypes, pcs):
    width = genotypes.shape[1]
    half, quarter = width // 2, width // 4
    s = lax.axis_index("snp")
    z = lax.axis_index("samp")
    chip = lax.div(s, 2)
    place = jnp.stack([lax.rem(s, 2), jnp.logical_or(z == 1, z == 2).astype(jnp.int32), chip ^ z])
    other_core = [(i, i ^ 1) for i in range(8)]

    def part(array, p):
        a, b = p * quarter, p * quarter + half
        return jnp.concatenate([array[:, a:a + quarter], array[:, b:b + quarter]], axis=1)

    design = jnp.concatenate([jnp.ones((1, width), jnp.float32), pcs], axis=0)
    design = jnp.pad(design, ((0, -DESIGN_ROWS % 8), (0, 0)))
    dosage = jnp.where(genotypes >= 0.0, genotypes, 0.0)
    cross_part = lax.dot_general(design, dosage, (((1,), (1,)), ((), ())), precision=HIGH)
    snps = cross_part.shape[1]
    mine = jnp.concatenate([cross_part, design], axis=1)
    middle = [(1, 2), (2, 1)]
    coded = [encode(part(genotypes, p)) for p in range(2)]
    coded = [after(c, mine) for c in coded]
    near = [lax.ppermute(c, "samp", [(i, i ^ 1) for i in range(4)]) for c in coded]
    across = [lax.ppermute(c, "samp", middle) for c in coded]
    end = [lax.ppermute(c, "samp", [(0, 3), (3, 0)]) for c in coded]
    far = [lax.ppermute(c, "samp", middle) for c in near]
    out = [lax.ppermute(c, "samp", [(1, 0), (2, 3)]) for c in across]

    theirs = [mine] + [lax.ppermute(mine, "samp", [(i, i ^ j) for i in range(4)]) for j in range(1, 4)]
    coef = coefficients(theirs, snps)
    designs = [padded(t[:, snps:]) for t in theirs]

    terms, keep_own, give_own = block_sums(place, coef, designs[0], own=genotypes)
    near_design = jnp.concatenate([part(designs[1], 0), part(designs[1], 1)], axis=1)
    keep_near, give_near = block_sums(place, coef, near_design, terms=terms, coded=near, sources=((0,), (1,)))
    got_own, got_near = [lax.ppermute(g, "snp", other_core) for g in (give_own, give_near)]
    parts = []
    for p in range(2):
        late_design = jnp.concatenate([part(designs[2], p), part(designs[3], p)], axis=1)
        keep, give = block_sums(place, coef, late_design, terms=terms, coded=(far[p], out[p], across[p], end[p]), sources=((0, 1), (2, 3)))
        got = lax.ppermute(give, "snp", other_core)
        mine, *sent = add_cores(place, p, keep_own, keep_near, keep, got_own, got_near, got)
        parts.append(mine)
        for d in range(1, 4):
            parts.append(lax.ppermute(sent[d - 1], "snp", [(i, i ^ (2 * d)) for i in range(8)]))
    return divide(parts)


def any_mesh(genotypes, pcs):
    width = genotypes.shape[1]
    design = jnp.concatenate([jnp.ones((1, width), jnp.float32), pcs], axis=0)
    observed = genotypes >= 0.0
    dosage = jnp.where(observed, genotypes, 0.0)
    cross_part = lax.dot_general(design, dosage, (((1,), (1,)), ((), ())), precision=HIGH)
    cross = lax.psum(cross_part, "samp")
    full = lax.all_gather(design, "samp", axis=1, tiled=True)
    fitted = lax.dot_general(solve_coef(full, cross), design, OVER_ROWS, precision=HIGH)
    own = resid_spread(dosage, observed, fitted)
    rows = lax.all_gather(jnp.stack(own), "samp", axis=2, tiled=True)
    sums = jnp.stack([product(rows[t], own[t]) for t in range(2)])
    return kinship(lax.psum_scatter(sums, "snp", scatter_dimension=1, tiled=True))


def solution(mesh):
    body = line_of_four if (mesh.shape["snp"], mesh.shape["samp"]) == (8, 4) else any_mesh
    in_specs = (P("snp", "samp"), P(None, "samp"))
    return jax.shard_map(body, mesh=mesh, in_specs=in_specs, out_specs=P("snp", "samp"), check_vma=False)
```

```python
import functools

import jax
import jax.numpy as jnp
from jax import lax
from jax.experimental import pallas as pl
from jax.experimental.pallas import tpu as pltpu
from jax.sharding import PartitionSpec as P

HIGH = lax.Precision.HIGHEST
LINK = jnp.float16
OVER_ROWS = (((0,), (0,)), ((), ()))
RANGE = 120.0
PAD = 32
VMEM_BYTES = 24 * 2**20
FRONT_BYTES = 60 * 2**20
DESIGN_ROWS = 21
STEP = 256
FREE = pl.CostEstimate(flops=0, bytes_accessed=0, transcendentals=0)


def solve_coef(design, cross):
    gram = jnp.dot(design, design.T, precision=HIGH)
    factor = jnp.linalg.cholesky(gram)
    return jax.scipy.linalg.cho_solve((factor, True), cross)


def encode(genotypes):
    return jnp.where(genotypes >= 0.0, jnp.exp2(RANGE * genotypes - RANGE), 0.0).astype(jnp.bfloat16)


def decode(coded):
    value = coded.astype(jnp.float32)
    observed = value > 0.0
    return jnp.log2(jnp.where(observed, value, 1.0)) * (1.0 / RANGE) + 1.0, observed


def thirds(x):
    a = x.astype(jnp.bfloat16)
    rest = x - a.astype(jnp.float32)
    b = rest.astype(jnp.bfloat16)
    return a, b, (rest - b.astype(jnp.float32)).astype(jnp.bfloat16)


def left_stack(x):
    a, b, c = thirds(x)
    return jnp.concatenate([a, a, b, b, a, c], axis=0)


def right_stack(y):
    a, b, c = thirds(y)
    return jnp.concatenate([a, b, a, b, c, a], axis=0)


def resid_spread(dosage, observed, fitted):
    twice = jnp.clip(fitted, 0.04, 1.96)
    product = twice * (2.0 - twice)
    resid = jnp.where(observed, dosage - twice, 0.0)
    spread = jnp.where(observed, 0.5 * jnp.sqrt(product), 0.0)
    return resid.astype(jnp.bfloat16), spread.astype(jnp.bfloat16)


def product(left, right):
    return lax.dot_general(left, right, OVER_ROWS, preferred_element_type=jnp.float32)


def cross_kernel(genotypes_ref, pcs_ref, mine_ref):
    count, width = genotypes_ref.shape
    k = pcs_ref.shape[0]
    rows = mine_ref.shape[0]
    snps = mine_ref.shape[1] - width
    genotypes = genotypes_ref[...]
    blank = jnp.zeros((rows - k - 1, width), jnp.float32)
    design = jnp.concatenate([jnp.ones((1, width), jnp.float32), pcs_ref[...], blank], axis=0)
    d = [t.astype(jnp.float32) for t in thirds(design)]
    stacked = jnp.concatenate(d + d[:1], axis=0).astype(jnp.bfloat16)
    g = thirds(jnp.where(genotypes >= 0.0, genotypes, 0.0))
    lanes = (((1,), (1,)), ((), ()))
    first, second, third = [lax.dot_general(t, stacked, lanes, preferred_element_type=jnp.float32) for t in g]
    cross = (first[:, 2 * rows:3 * rows] + second[:, rows:2 * rows] + third[:, :rows]) + (first[:, rows:2 * rows] + second[:, :rows])
    cross = cross + first[:, :rows]
    step = pl.program_id(0)
    mine_ref[:, pl.ds(pl.multiple_of(step * count, count), count)] = cross.T

    @pl.when(step == 0)
    def _():
        mine_ref[:, snps:] = design


def cross_part(genotypes, pcs):
    snps, width = genotypes.shape
    rows = DESIGN_ROWS + -DESIGN_ROWS % 8
    return pl.pallas_call(
        cross_kernel,
        grid=(snps // STEP,),
        out_shape=jax.ShapeDtypeStruct((rows, snps + width), jnp.float32),
        in_specs=[pl.BlockSpec((STEP, width), lambda i: (i, 0)), pl.BlockSpec(pcs.shape, lambda i: (0, 0))],
        out_specs=pl.BlockSpec((rows, snps + width), lambda i: (0, 0)),
        compiler_params=pltpu.CompilerParams(vmem_limit_bytes=FRONT_BYTES),
        cost_estimate=FREE,
    )(genotypes, pcs)


def coef_kernel(cuts, mine_ref, a_ref, b_ref, c_ref, coef_ref, own_ref, near_ref, late_ref):
    rows, snps = mine_ref.shape[0], coef_ref.shape[1]
    across_lanes = (((1,), (1,)), ((), ()))
    cross = mine_ref[:, :snps] + a_ref[:, :snps] + b_ref[:, :snps] + c_ref[:, :snps]
    gram = jnp.zeros((rows, rows), jnp.float32)
    blank = jnp.zeros((PAD - rows, near_ref.shape[1]), jnp.float32)
    half = near_ref.shape[1] // 2
    for j, ref in enumerate((mine_ref, a_ref, b_ref, c_ref)):
        design = ref[:, snps:]
        gram = gram + lax.dot_general(design, design, across_lanes, precision=HIGH, preferred_element_type=jnp.float32)
        if j > 0:
            design = jnp.concatenate([design[:, at:at + n] for first, n in cuts for at in (first, first + half)], axis=1)
        stacked = right_stack(jnp.concatenate([design, blank], axis=0))
        if j < 2:
            (own_ref, near_ref)[j][...] = stacked
        else:
            late_ref[j - 2] = stacked
    row = lax.broadcasted_iota(jnp.int32, (rows, rows), 0)
    unit = (row == lax.broadcasted_iota(jnp.int32, (rows, rows), 1)).astype(jnp.float32)
    gram = gram + jnp.where(row >= DESIGN_ROWS, unit, 0.0)
    left, inverse = gram, unit
    for j in range(DESIGN_ROWS):
        pivot = 1.0 / left[j:j + 1, j:j + 1]
        factor = (left[:, j:j + 1] - unit[:, j:j + 1]) * pivot
        left, inverse = left - factor * left[j:j + 1, :], inverse - factor * inverse[j:j + 1, :]
    coef = jnp.dot(inverse, cross, precision=HIGH, preferred_element_type=jnp.float32)
    rest = cross - jnp.dot(gram, coef, precision=HIGH, preferred_element_type=jnp.float32)
    coef = coef + jnp.dot(inverse, rest, precision=HIGH, preferred_element_type=jnp.float32)
    coef_ref[...] = left_stack(jnp.concatenate([coef, jnp.zeros((PAD - rows, snps), jnp.float32)], axis=0))


def coefficients(theirs, snps, cuts):
    vmem = pl.BlockSpec(memory_space=pltpu.VMEM)
    width = theirs[0].shape[1] - snps
    shapes = [(6 * PAD, snps), (6 * PAD, width), (6 * PAD, width), (2, 6 * PAD, width)]
    return pl.pallas_call(
        functools.partial(coef_kernel, cuts),
        out_shape=tuple(jax.ShapeDtypeStruct(shape, jnp.bfloat16) for shape in shapes),
        in_specs=[vmem] * 4,
        out_specs=(vmem,) * 4,
        compiler_params=pltpu.CompilerParams(vmem_limit_bytes=VMEM_BYTES),
        cost_estimate=pl.CostEstimate(flops=10**10, bytes_accessed=0, transcendentals=0),
    )(*theirs)


def pack(sums):
    size = jnp.exp2(8.0 * jnp.log2(jnp.maximum(jnp.abs(sums), 1e-30)) + 20.0)
    return jnp.where(sums < 0.0, -size, size).astype(jnp.bfloat16)


def unpack(packed):
    value = packed.astype(jnp.float32)
    size = jnp.abs(value)
    sums = jnp.exp2(jnp.log2(jnp.where(size > 0.0, size, 1.0)) * 0.125 - 2.5)
    return jnp.where(size > 0.0, jnp.where(value < 0.0, -sums, sums), 0.0)


def own_kernel(place_ref, coef_ref, design_ref, own_ref, terms_ref, keep_ref, give_ref):
    half = keep_ref.shape[1]
    snps = coef_ref.shape[1]

    def terms(k, _):
        at = pl.ds(pl.multiple_of(k * STEP, STEP), STEP)
        dosage = own_ref[at, :]
        fitted = product(coef_ref[:, at], design_ref[...])
        terms_ref[0, at, :], terms_ref[1, at, :] = resid_spread(dosage, dosage >= 0.0, fitted)
        return 0

    lax.fori_loop(0, snps // STEP, terms, 0)
    first_core = place_ref[0] == 0
    for t in range(2):
        a, b = [product(terms_ref[t, :, h * half:(h + 1) * half], terms_ref[t]) for h in range(2)]
        keep_ref[t] = jnp.where(first_core, a, b)
        give_ref[t] = pack(jnp.where(first_core, b, a))


def block_kernel(groups, place_ref, coef_ref, design_ref, terms_ref, *refs):
    *coded, keep_ref, give_ref, rows_ref = refs
    snps = coef_ref.shape[1]

    def terms(k, _):
        at = pl.ds(pl.multiple_of(k * STEP, STEP), STEP)
        first = 0
        for choices, design, count, _ in groups:
            here = slice(first, first + 2 * count)
            values = [coded[i][at, c:c + 2 * count] for i, c in choices]
            value = values[0] if len(values) == 1 else jnp.where(place_ref[1] == 1, values[0], values[1])
            dosage, observed = decode(value)
            fitted = product(coef_ref[:, at], design_ref[design])
            rows_ref[0, at, here], rows_ref[1, at, here] = resid_spread(dosage, observed, fitted)
            first += 2 * count
        return 0

    lax.fori_loop(0, snps // STEP, terms, 0)
    first_core = place_ref[0] == 0
    first = 0
    for _, _, count, target in groups:
        for t in range(2):
            sums = product(rows_ref[t, :, first:first + 2 * count], terms_ref[t])
            a, b = sums[:count], sums[count:]
            keep_ref[target(t)] = jnp.where(first_core, a, b)
            give_ref[target(t)] = pack(jnp.where(first_core, b, a))
        first += 2 * count


def block_sums(place, coef, design, sums, own=None, terms=None, coded=(), groups=()):
    snps = coef.shape[1]
    vmem = pl.BlockSpec(memory_space=pltpu.VMEM)
    out = (jax.ShapeDtypeStruct(sums, jnp.float32), jax.ShapeDtypeStruct(sums, jnp.bfloat16))
    if own is not None:
        kernel, operands, scratch = own_kernel, (place, coef, design, own), []
        out = (jax.ShapeDtypeStruct((2,) + own.shape, jnp.bfloat16),) + out
    else:
        kernel, operands = functools.partial(block_kernel, groups), (place, coef, design, terms, *coded)
        scratch = [pltpu.VMEM((2, snps, sum(2 * group[2] for group in groups)), jnp.bfloat16)]
    return pl.pallas_call(
        kernel,
        out_shape=out,
        in_specs=[pl.BlockSpec(memory_space=pltpu.SMEM)] + [vmem] * (len(operands) - 1),
        out_specs=tuple(vmem for _ in out),
        scratch_shapes=scratch,
        compiler_params=pltpu.CompilerParams(vmem_limit_bytes=VMEM_BYTES),
        cost_estimate=FREE,
    )(*operands)


def add_kernel(first, place_ref, own_ref, near_ref, late_ref, got_own_ref, got_near_ref, got_late_ref, mine_ref, *refs):
    *sent, sums = refs
    here = slice(first, first + mine_ref.shape[1])
    sums[0] = own_ref[:, here] + unpack(got_own_ref[:, here])
    sums[1] = near_ref[:, here] + unpack(got_near_ref[:, here])
    for i in range(2):
        sums[2 + i] = late_ref[i] + unpack(got_late_ref[i])
    mine_ref[...] = sums[place_ref[2]]
    for d, ref in enumerate(sent, 1):
        ref[...] = pack(sums[jnp.bitwise_xor(place_ref[2], d)])


def add_cores(place, first, *operands):
    shape = operands[2].shape[1:]
    vmem = pl.BlockSpec(memory_space=pltpu.VMEM)
    return pl.pallas_call(
        functools.partial(add_kernel, first),
        out_shape=(jax.ShapeDtypeStruct(shape, jnp.float32),) + (jax.ShapeDtypeStruct(shape, jnp.bfloat16),) * 3,
        in_specs=[pl.BlockSpec(memory_space=pltpu.SMEM)] + [vmem] * len(operands),
        out_specs=(vmem,) * 4,
        scratch_shapes=[pltpu.VMEM((4,) + shape, jnp.float32)],
        compiler_params=pltpu.CompilerParams(vmem_limit_bytes=VMEM_BYTES),
        cost_estimate=FREE,
    )(place, *operands)


def divide_kernel(*refs):
    *parts, out_ref = refs
    first = 0
    for p in range(len(parts) // 4):
        mine, *got = parts[4 * p:4 * p + 4]
        count = mine.shape[1]
        sums = [mine[t] + unpack(got[0][t]) + unpack(got[1][t]) + unpack(got[2][t]) for t in range(2)]
        out_ref[first:first + count, :] = sums[0] / (4.0 * sums[1])
        first += count


def divide(parts):
    width = parts[0].shape[2]
    vmem = pl.BlockSpec(memory_space=pltpu.VMEM)
    return pl.pallas_call(
        divide_kernel,
        out_shape=jax.ShapeDtypeStruct((sum(m.shape[1] for m in parts[::4]), width), jnp.float32),
        in_specs=[vmem] * len(parts),
        out_specs=vmem,
        compiler_params=pltpu.CompilerParams(vmem_limit_bytes=VMEM_BYTES),
        cost_estimate=FREE,
    )(*parts)


def kinship(sums):
    return sums[0] / (4.0 * sums[1])


def after(value, *earlier):
    return lax.optimization_barrier((value, *earlier))[0]


def line_of_four(genotypes, pcs):
    width = genotypes.shape[1]
    half = width // 2
    s = lax.axis_index("snp")
    z = lax.axis_index("samp")
    chip = lax.div(s, 2)
    inner = jnp.logical_or(z == 1, z == 2)
    place = jnp.stack([lax.rem(s, 2), inner.astype(jnp.int32), chip ^ z])
    other_core = [(i, i ^ 1) for i in range(8)]
    cuts, pieces = ((0, half // 2), (half // 2, half // 4), (3 * half // 4, half // 4)), ((0,), (1, 2))
    mine = cross_part(genotypes, pcs)
    snps = genotypes.shape[0]
    theirs = [mine] + [lax.ppermute(mine, "samp", [(i, i ^ j) for i in range(4)]) for j in range(1, 4)]
    coef, design_own, design_near, design_late = coefficients(theirs, snps, cuts)

    coded = []
    for piece in pieces:
        columns = [genotypes[:, at:at + n] for p in piece for first, n in cuts[p:p + 1] for at in (first, first + half)]
        coded.append(encode(after(jnp.concatenate(columns, axis=1), mine)))
    near = [lax.ppermute(c, "samp", [(i, i ^ 1) for i in range(4)]) for c in coded]
    across = [lax.ppermute(c, "samp", [(1, 2), (2, 1)]) for c in coded]
    held, begin = {}, {}
    for i, piece in enumerate(pieces):
        at = 0
        for p in piece:
            held[p] = (i, at)
            at += 2 * cuts[p][1]
    start = 0
    for p, (_, count) in enumerate(cuts):
        begin[p] = start
        start += 2 * count

    sums = (2, half, width)
    terms, keep_own, give_own = block_sums(place, coef, design_own, sums, own=genotypes)
    groups = [
        (((held[p]),), (slice(None), slice(begin[p], begin[p] + 2 * n)), n, lambda t, first=first, n=n: (t, slice(first, first + n)))
        for p, (first, n) in enumerate(cuts)
    ]
    keep_near, give_near = block_sums(place, coef, design_near, sums, terms=terms, coded=near, groups=groups)
    got_own, got_near = [lax.ppermute(g, "snp", other_core) for g in (give_own, give_near)]
    totals, gates = [], [(), (), ()]
    for p, (first, count) in enumerate(cuts):
        i, at = held[p]
        cols = slice(at, at + 2 * count)
        ready = jnp.where(inner, near[i][:, cols], coded[i][:, cols])
        again = across[i][:, cols]
        if gates[p]:
            ready, again = [after(r, *gates[p]) for r in (ready, again)]
        far = lax.ppermute(ready, "samp", [(1, 2), (2, 1), (0, 3), (3, 0)])
        out = lax.ppermute(again, "samp", [(1, 0), (2, 3)])
        where = [(g, slice(None), slice(begin[p], begin[p] + 2 * count)) for g in range(2)]
        groups = [
            (choices, where[g], count, lambda t, g=g: (g, t)) for g, choices in enumerate((((0, 0), (1, 0)), ((2, at), (0, 0))))
        ]
        if p == 2:
            terms = after(terms, *totals[1:4])
        keep, give = block_sums(place, coef, design_late, (2, 2, count, width), terms=terms, coded=(far, out, across[i]), groups=groups)
        got = lax.ppermute(give, "snp", other_core)
        kept, *sent = add_cores(place, first, keep_own, keep_near, keep, got_own, got_near, got)
        if p == 0:
            gates[2] = (kept,)
        totals.append(kept)
        for d in range(1, 4):
            totals.append(lax.ppermute(sent[d - 1], "snp", [(i, i ^ (2 * d)) for i in range(8)]))
    return divide(totals)


def any_mesh(genotypes, pcs):
    width = genotypes.shape[1]
    design = jnp.concatenate([jnp.ones((1, width), jnp.float32), pcs], axis=0)
    observed = genotypes >= 0.0
    dosage = jnp.where(observed, genotypes, 0.0)
    cross_part = lax.dot_general(design, dosage, (((1,), (1,)), ((), ())), precision=HIGH)
    cross = lax.psum(cross_part, "samp")
    full = lax.all_gather(design, "samp", axis=1, tiled=True)
    fitted = lax.dot_general(solve_coef(full, cross), design, OVER_ROWS, precision=HIGH)
    own = resid_spread(dosage, observed, fitted)
    rows = lax.all_gather(jnp.stack(own), "samp", axis=2, tiled=True)
    sums = jnp.stack([product(rows[t], own[t]) for t in range(2)])
    return kinship(lax.psum_scatter(sums, "snp", scatter_dimension=1, tiled=True))


def solution(mesh):
    body = line_of_four if (mesh.shape["snp"], mesh.shape["samp"]) == (8, 4) else any_mesh
    in_specs = (P("snp", "samp"), P(None, "samp"))
    return jax.shard_map(body, mesh=mesh, in_specs=in_specs, out_specs=P("snp", "samp"), check_vma=False)
```

```python
import functools

import jax
import jax.numpy as jnp
from jax import lax
from jax.experimental import pallas as pl
from jax.experimental.pallas import tpu as pltpu
from jax.sharding import PartitionSpec as P

HIGH = lax.Precision.HIGHEST
LINK = jnp.float16
OVER_ROWS = (((0,), (0,)), ((), ()))
RANGE = 120.0
PAD = 32
VMEM_BYTES = 24 * 2**20
FRONT_BYTES = 60 * 2**20
DESIGN_ROWS = 21
STEP = 256
CROSS = 512
FREE = pl.CostEstimate(flops=0, bytes_accessed=0, transcendentals=0)


def solve_coef(design, cross):
    gram = jnp.dot(design, design.T, precision=HIGH)
    factor = jnp.linalg.cholesky(gram)
    return jax.scipy.linalg.cho_solve((factor, True), cross)


def encode(genotypes):
    return jnp.where(genotypes >= 0.0, jnp.exp2(RANGE * genotypes - RANGE), 0.0).astype(jnp.bfloat16)


def decode(coded):
    value = coded.astype(jnp.float32)
    observed = value > 0.0
    return jnp.log2(jnp.where(observed, value, 1.0)) * (1.0 / RANGE) + 1.0, observed


def thirds(x):
    a = x.astype(jnp.bfloat16)
    rest = x - a.astype(jnp.float32)
    b = rest.astype(jnp.bfloat16)
    return a, b, (rest - b.astype(jnp.float32)).astype(jnp.bfloat16)


def left_stack(x):
    a, b, c = thirds(x)
    return jnp.concatenate([a, a, b, b, a, c], axis=0)


def right_stack(y):
    a, b, c = thirds(y)
    return jnp.concatenate([a, b, a, b, c, a], axis=0)


def resid_spread(dosage, observed, fitted):
    twice = jnp.clip(fitted, 0.04, 1.96)
    product = twice * (2.0 - twice)
    resid = jnp.where(observed, dosage - twice, 0.0)
    spread = jnp.where(observed, 0.5 * jnp.sqrt(product), 0.0)
    return resid.astype(jnp.bfloat16), spread.astype(jnp.bfloat16)


def product(left, right):
    return lax.dot_general(left, right, OVER_ROWS, preferred_element_type=jnp.float32)


def cross_kernel(genotypes_ref, pcs_ref, mine_ref):
    count, width = genotypes_ref.shape
    k = pcs_ref.shape[0]
    rows = mine_ref.shape[0]
    snps = mine_ref.shape[1] - width
    genotypes = genotypes_ref[...]
    blank = jnp.zeros((rows - k - 1, width), jnp.float32)
    design = jnp.concatenate([jnp.ones((1, width), jnp.float32), pcs_ref[...], blank], axis=0)
    d = [t.astype(jnp.float32) for t in thirds(design)]
    stacked = jnp.concatenate(d + d[:1], axis=0).astype(jnp.bfloat16)
    g = thirds(jnp.where(genotypes >= 0.0, genotypes, 0.0))
    lanes = (((1,), (1,)), ((), ()))
    first, second, third = [lax.dot_general(t, stacked, lanes, preferred_element_type=jnp.float32) for t in g]
    cross = (first[:, 2 * rows:3 * rows] + second[:, rows:2 * rows] + third[:, :rows]) + (first[:, rows:2 * rows] + second[:, :rows])
    cross = cross + first[:, :rows]
    step = pl.program_id(0)
    mine_ref[:, pl.ds(pl.multiple_of(step * count, count), count)] = cross.T

    @pl.when(step == 0)
    def _():
        mine_ref[:, snps:] = design


def cross_part(genotypes, pcs):
    snps, width = genotypes.shape
    rows = DESIGN_ROWS + -DESIGN_ROWS % 8
    return pl.pallas_call(
        cross_kernel,
        grid=(snps // CROSS,),
        out_shape=jax.ShapeDtypeStruct((rows, snps + width), jnp.float32),
        in_specs=[pl.BlockSpec((CROSS, width), lambda i: (i, 0)), pl.BlockSpec(pcs.shape, lambda i: (0, 0))],
        out_specs=pl.BlockSpec((rows, snps + width), lambda i: (0, 0)),
        compiler_params=pltpu.CompilerParams(vmem_limit_bytes=FRONT_BYTES),
        cost_estimate=FREE,
    )(genotypes, pcs)


def coef_kernel(cuts, pair_ref, got_ref, coef_ref, own_ref, near_ref, late_ref):
    rows, (snps, width) = pair_ref.shape[0], (coef_ref.shape[1], near_ref.shape[1])
    across_lanes = (((1,), (1,)), ((), ()))
    cross = pair_ref[:, :snps] + got_ref[:, :snps]
    gram = jnp.zeros((rows, rows), jnp.float32)
    blank = jnp.zeros((PAD - rows, width), jnp.float32)
    for j, ref in enumerate((pair_ref, pair_ref, got_ref, got_ref)):
        design = ref[:, snps + j % 2 * width:snps + (j % 2 + 1) * width]
        gram = gram + lax.dot_general(design, design, across_lanes, precision=HIGH, preferred_element_type=jnp.float32)
        if j > 0:
            design = jnp.concatenate([design[:, at:at + n] for first, n in cuts for at in (first, first + width // 2)], axis=1)
        stacked = right_stack(jnp.concatenate([design, blank], axis=0))
        if j < 2:
            (own_ref, near_ref)[j][...] = stacked
        else:
            late_ref[j - 2] = stacked
    row = lax.broadcasted_iota(jnp.int32, (rows, rows), 0)
    unit = (row == lax.broadcasted_iota(jnp.int32, (rows, rows), 1)).astype(jnp.float32)
    gram = gram + jnp.where(row >= DESIGN_ROWS, unit, 0.0)
    left, inverse = gram, unit
    for j in range(DESIGN_ROWS):
        pivot = 1.0 / left[j:j + 1, j:j + 1]
        factor = (left[:, j:j + 1] - unit[:, j:j + 1]) * pivot
        left, inverse = left - factor * left[j:j + 1, :], inverse - factor * inverse[j:j + 1, :]
    coef = jnp.dot(inverse, cross, precision=HIGH, preferred_element_type=jnp.float32)
    rest = cross - jnp.dot(gram, coef, precision=HIGH, preferred_element_type=jnp.float32)
    coef = coef + jnp.dot(inverse, rest, precision=HIGH, preferred_element_type=jnp.float32)
    coef_ref[...] = left_stack(jnp.concatenate([coef, jnp.zeros((PAD - rows, snps), jnp.float32)], axis=0))


def coefficients(pair, got, snps, cuts):
    vmem = pl.BlockSpec(memory_space=pltpu.VMEM)
    width = (pair.shape[1] - snps) // 2
    shapes = [(6 * PAD, snps), (6 * PAD, width), (6 * PAD, width), (2, 6 * PAD, width)]
    return pl.pallas_call(
        functools.partial(coef_kernel, cuts),
        out_shape=tuple(jax.ShapeDtypeStruct(shape, jnp.bfloat16) for shape in shapes),
        in_specs=[vmem] * 2,
        out_specs=(vmem,) * 4,
        compiler_params=pltpu.CompilerParams(vmem_limit_bytes=VMEM_BYTES),
        cost_estimate=pl.CostEstimate(flops=10**10, bytes_accessed=0, transcendentals=0),
    )(pair, got)


def pack(sums):
    size = jnp.exp2(8.0 * jnp.log2(jnp.maximum(jnp.abs(sums), 1e-30)) + 20.0)
    return jnp.where(sums < 0.0, -size, size).astype(jnp.bfloat16)


def unpack(packed):
    value = packed.astype(jnp.float32)
    size = jnp.abs(value)
    sums = jnp.exp2(jnp.log2(jnp.where(size > 0.0, size, 1.0)) * 0.125 - 2.5)
    return jnp.where(size > 0.0, jnp.where(value < 0.0, -sums, sums), 0.0)


def own_kernel(place_ref, coef_ref, design_ref, own_ref, terms_ref, keep_ref, give_ref):
    half = keep_ref.shape[1]
    snps = coef_ref.shape[1]

    def terms(k, _):
        at = pl.ds(pl.multiple_of(k * STEP, STEP), STEP)
        dosage = own_ref[at, :]
        fitted = product(coef_ref[:, at], design_ref[...])
        terms_ref[0, at, :], terms_ref[1, at, :] = resid_spread(dosage, dosage >= 0.0, fitted)
        return 0

    lax.fori_loop(0, snps // STEP, terms, 0)
    first_core = place_ref[0] == 0
    for t in range(2):
        a, b = [product(terms_ref[t, :, h * half:(h + 1) * half], terms_ref[t]) for h in range(2)]
        keep_ref[t] = jnp.where(first_core, a, b)
        give_ref[t] = pack(jnp.where(first_core, b, a))


def block_kernel(groups, place_ref, coef_ref, design_ref, terms_ref, *refs):
    *coded, keep_ref, give_ref, rows_ref = refs
    snps = coef_ref.shape[1]

    def terms(k, _):
        at = pl.ds(pl.multiple_of(k * STEP, STEP), STEP)
        first = 0
        for choices, design, count, _ in groups:
            here = slice(first, first + 2 * count)
            values = [coded[i][at, c:c + 2 * count] for i, c in choices]
            value = values[0] if len(values) == 1 else jnp.where(place_ref[1] == 1, values[0], values[1])
            dosage, observed = decode(value)
            fitted = product(coef_ref[:, at], design_ref[design])
            rows_ref[0, at, here], rows_ref[1, at, here] = resid_spread(dosage, observed, fitted)
            first += 2 * count
        return 0

    lax.fori_loop(0, snps // STEP, terms, 0)
    first_core = place_ref[0] == 0
    first = 0
    for _, _, count, target in groups:
        for t in range(2):
            sums = product(rows_ref[t, :, first:first + 2 * count], terms_ref[t])
            a, b = sums[:count], sums[count:]
            keep_ref[target(t)] = jnp.where(first_core, a, b)
            give_ref[target(t)] = pack(jnp.where(first_core, b, a))
        first += 2 * count


def block_sums(place, coef, design, sums, own=None, terms=None, coded=(), groups=()):
    snps = coef.shape[1]
    vmem = pl.BlockSpec(memory_space=pltpu.VMEM)
    out = (jax.ShapeDtypeStruct(sums, jnp.float32), jax.ShapeDtypeStruct(sums, jnp.bfloat16))
    if own is not None:
        kernel, operands, scratch = own_kernel, (place, coef, design, own), []
        out = (jax.ShapeDtypeStruct((2,) + own.shape, jnp.bfloat16),) + out
    else:
        kernel, operands = functools.partial(block_kernel, groups), (place, coef, design, terms, *coded)
        scratch = [pltpu.VMEM((2, snps, sum(2 * group[2] for group in groups)), jnp.bfloat16)]
    return pl.pallas_call(
        kernel,
        out_shape=out,
        in_specs=[pl.BlockSpec(memory_space=pltpu.SMEM)] + [vmem] * (len(operands) - 1),
        out_specs=tuple(vmem for _ in out),
        scratch_shapes=scratch,
        compiler_params=pltpu.CompilerParams(vmem_limit_bytes=VMEM_BYTES),
        cost_estimate=FREE,
    )(*operands)


def add_kernel(first, place_ref, own_ref, near_ref, late_ref, got_own_ref, got_near_ref, got_late_ref, mine_ref, *refs):
    *sent, sums = refs
    here = slice(first, first + mine_ref.shape[1])
    sums[0] = own_ref[:, here] + unpack(got_own_ref[:, here])
    sums[1] = near_ref[:, here] + unpack(got_near_ref[:, here])
    for i in range(2):
        sums[2 + i] = late_ref[i] + unpack(got_late_ref[i])
    mine_ref[...] = sums[place_ref[2]]
    for d, ref in enumerate(sent, 1):
        ref[...] = pack(sums[jnp.bitwise_xor(place_ref[2], d)])


def add_cores(place, first, *operands):
    shape = operands[2].shape[1:]
    vmem = pl.BlockSpec(memory_space=pltpu.VMEM)
    return pl.pallas_call(
        functools.partial(add_kernel, first),
        out_shape=(jax.ShapeDtypeStruct(shape, jnp.float32),) + (jax.ShapeDtypeStruct(shape, jnp.bfloat16),) * 3,
        in_specs=[pl.BlockSpec(memory_space=pltpu.SMEM)] + [vmem] * len(operands),
        out_specs=(vmem,) * 4,
        scratch_shapes=[pltpu.VMEM((4,) + shape, jnp.float32)],
        compiler_params=pltpu.CompilerParams(vmem_limit_bytes=VMEM_BYTES),
        cost_estimate=FREE,
    )(place, *operands)


def divide_kernel(*refs):
    *parts, out_ref = refs
    first = 0
    for p in range(len(parts) // 4):
        mine, *got = parts[4 * p:4 * p + 4]
        count = mine.shape[1]
        sums = [mine[t] + unpack(got[0][t]) + unpack(got[1][t]) + unpack(got[2][t]) for t in range(2)]
        out_ref[first:first + count, :] = sums[0] / (4.0 * sums[1])
        first += count


def divide(parts):
    width = parts[0].shape[2]
    vmem = pl.BlockSpec(memory_space=pltpu.VMEM)
    return pl.pallas_call(
        divide_kernel,
        out_shape=jax.ShapeDtypeStruct((sum(m.shape[1] for m in parts[::4]), width), jnp.float32),
        in_specs=[vmem] * len(parts),
        out_specs=vmem,
        compiler_params=pltpu.CompilerParams(vmem_limit_bytes=VMEM_BYTES),
        cost_estimate=FREE,
    )(*parts)


def kinship(sums):
    return sums[0] / (4.0 * sums[1])


def after(value, *earlier):
    return lax.optimization_barrier((value, *earlier))[0]


def line_of_four(genotypes, pcs):
    width = genotypes.shape[1]
    half = width // 2
    s = lax.axis_index("snp")
    z = lax.axis_index("samp")
    chip = lax.div(s, 2)
    inner = jnp.logical_or(z == 1, z == 2)
    place = jnp.stack([lax.rem(s, 2), inner.astype(jnp.int32), chip ^ z])
    other_core = [(i, i ^ 1) for i in range(8)]
    cuts, pieces = ((0, half // 2), (half // 2, half // 4), (3 * half // 4, half // 4)), ((0,), (1, 2))
    mine = cross_part(genotypes, pcs)
    snps = genotypes.shape[0]
    other = lax.ppermute(mine, "samp", [(i, i ^ 1) for i in range(4)])
    pair = jnp.concatenate([mine[:, :snps] + other[:, :snps], mine[:, snps:], other[:, snps:]], axis=1)
    got = lax.ppermute(pair, "samp", [(i, i ^ 2) for i in range(4)])
    coef, design_own, design_near, design_late = coefficients(pair, got, snps, cuts)

    coded = []
    for piece in pieces:
        columns = [genotypes[:, at:at + n] for p in piece for first, n in cuts[p:p + 1] for at in (first, first + half)]
        coded.append(encode(after(jnp.concatenate(columns, axis=1), mine if not coded else pair)))
    near = [lax.ppermute(c, "samp", [(i, i ^ 1) for i in range(4)]) for c in coded]
    across = [lax.ppermute(c, "samp", [(1, 2), (2, 1)]) for c in coded]
    held, begin = {}, {}
    for i, piece in enumerate(pieces):
        at = 0
        for p in piece:
            held[p] = (i, at)
            at += 2 * cuts[p][1]
    start = 0
    for p, (_, count) in enumerate(cuts):
        begin[p] = start
        start += 2 * count

    sums = (2, half, width)
    terms, keep_own, give_own = block_sums(place, coef, design_own, sums, own=genotypes)
    groups = [
        (((held[p]),), (slice(None), slice(begin[p], begin[p] + 2 * n)), n, lambda t, first=first, n=n: (t, slice(first, first + n)))
        for p, (first, n) in enumerate(cuts)
    ]
    keep_near, give_near = block_sums(place, coef, design_near, sums, terms=terms, coded=near, groups=groups)
    got_own, got_near = [lax.ppermute(g, "snp", other_core) for g in (give_own, give_near)]
    totals, gates = [], [(), (), ()]
    for p, (first, count) in enumerate(cuts):
        i, at = held[p]
        cols = slice(at, at + 2 * count)
        ready = jnp.where(inner, near[i][:, cols], coded[i][:, cols])
        again = across[i][:, cols]
        if gates[p]:
            ready, again = [after(r, *gates[p]) for r in (ready, again)]
        far = lax.ppermute(ready, "samp", [(1, 2), (2, 1), (0, 3), (3, 0)])
        out = lax.ppermute(again, "samp", [(1, 0), (2, 3)])
        where = [(g, slice(None), slice(begin[p], begin[p] + 2 * count)) for g in range(2)]
        groups = [
            (choices, where[g], count, lambda t, g=g: (g, t)) for g, choices in enumerate((((0, 0), (1, 0)), ((2, at), (0, 0))))
        ]
        if p == 2:
            terms = after(terms, *totals[1:4])
        keep, give = block_sums(place, coef, design_late, (2, 2, count, width), terms=terms, coded=(far, out, across[i]), groups=groups)
        got = lax.ppermute(give, "snp", other_core)
        kept, *sent = add_cores(place, first, keep_own, keep_near, keep, got_own, got_near, got)
        if p == 0:
            gates[2] = (kept,)
        totals.append(kept)
        for d in range(1, 4):
            totals.append(lax.ppermute(sent[d - 1], "snp", [(i, i ^ (2 * d)) for i in range(8)]))
    return divide(totals)


def any_mesh(genotypes, pcs):
    width = genotypes.shape[1]
    design = jnp.concatenate([jnp.ones((1, width), jnp.float32), pcs], axis=0)
    observed = genotypes >= 0.0
    dosage = jnp.where(observed, genotypes, 0.0)
    cross_part = lax.dot_general(design, dosage, (((1,), (1,)), ((), ())), precision=HIGH)
    cross = lax.psum(cross_part, "samp")
    full = lax.all_gather(design, "samp", axis=1, tiled=True)
    fitted = lax.dot_general(solve_coef(full, cross), design, OVER_ROWS, precision=HIGH)
    own = resid_spread(dosage, observed, fitted)
    rows = lax.all_gather(jnp.stack(own), "samp", axis=2, tiled=True)
    sums = jnp.stack([product(rows[t], own[t]) for t in range(2)])
    return kinship(lax.psum_scatter(sums, "snp", scatter_dimension=1, tiled=True))


def solution(mesh):
    body = line_of_four if (mesh.shape["snp"], mesh.shape["samp"]) == (8, 4) else any_mesh
    in_specs = (P("snp", "samp"), P(None, "samp"))
    return jax.shard_map(body, mesh=mesh, in_specs=in_specs, out_specs=P("snp", "samp"), check_vma=False)
```

```python
import functools

import jax
import jax.numpy as jnp
from jax import lax
from jax.experimental import pallas as pl
from jax.experimental.pallas import tpu as pltpu
from jax.sharding import PartitionSpec as P

HIGH = lax.Precision.HIGHEST
LINK = jnp.float16
OVER_ROWS = (((0,), (0,)), ((), ()))
RANGE = 120.0
PAD = 32
VMEM_BYTES = 24 * 2**20
FRONT_BYTES = 60 * 2**20
DESIGN_ROWS = 21
STEP = 256
CROSS = 512
FREE = pl.CostEstimate(flops=0, bytes_accessed=0, transcendentals=0)


def solve_coef(design, cross):
    gram = jnp.dot(design, design.T, precision=HIGH)
    factor = jnp.linalg.cholesky(gram)
    return jax.scipy.linalg.cho_solve((factor, True), cross)


def encode(genotypes):
    return jnp.where(genotypes >= 0.0, jnp.exp2(RANGE * genotypes - RANGE), 0.0).astype(jnp.bfloat16)


def decode(coded):
    value = coded.astype(jnp.float32)
    observed = value > 0.0
    return jnp.log2(jnp.where(observed, value, 1.0)) * (1.0 / RANGE) + 1.0, observed


def thirds(x):
    a = x.astype(jnp.bfloat16)
    rest = x - a.astype(jnp.float32)
    b = rest.astype(jnp.bfloat16)
    return a, b, (rest - b.astype(jnp.float32)).astype(jnp.bfloat16)


def left_stack(x):
    a, b, c = thirds(x)
    return jnp.concatenate([a, a, b, b, a, c], axis=0)


def right_stack(y):
    a, b, c = thirds(y)
    return jnp.concatenate([a, b, a, b, c, a], axis=0)


def resid_spread(dosage, observed, fitted):
    twice = jnp.clip(fitted, 0.04, 1.96)
    product = twice * (2.0 - twice)
    resid = jnp.where(observed, dosage - twice, 0.0)
    spread = jnp.where(observed, 0.5 * jnp.sqrt(product), 0.0)
    return resid.astype(jnp.bfloat16), spread.astype(jnp.bfloat16)


def product(left, right):
    return lax.dot_general(left, right, OVER_ROWS, preferred_element_type=jnp.float32)


def cross_kernel(genotypes_ref, pcs_ref, mine_ref):
    count, width = genotypes_ref.shape
    k = pcs_ref.shape[0]
    rows = mine_ref.shape[0]
    snps = mine_ref.shape[1] - width
    genotypes = genotypes_ref[...]
    blank = jnp.zeros((rows - k - 1, width), jnp.float32)
    design = jnp.concatenate([jnp.ones((1, width), jnp.float32), pcs_ref[...], blank], axis=0)
    d = [t.astype(jnp.float32) for t in thirds(design)]
    stacked = jnp.concatenate(d + d[:1], axis=0).astype(jnp.bfloat16)
    g = thirds(jnp.where(genotypes >= 0.0, genotypes, 0.0))
    lanes = (((1,), (1,)), ((), ()))
    first, second, third = [lax.dot_general(t, stacked, lanes, preferred_element_type=jnp.float32) for t in g]
    cross = (first[:, 2 * rows:3 * rows] + second[:, rows:2 * rows] + third[:, :rows]) + (first[:, rows:2 * rows] + second[:, :rows])
    cross = cross + first[:, :rows]
    step = pl.program_id(0)
    mine_ref[:, pl.ds(pl.multiple_of(step * count, count), count)] = cross.T

    @pl.when(step == 0)
    def _():
        mine_ref[:, snps:] = design


def cross_part(genotypes, pcs):
    snps, width = genotypes.shape
    rows = DESIGN_ROWS + -DESIGN_ROWS % 8
    return pl.pallas_call(
        cross_kernel,
        grid=(snps // CROSS,),
        out_shape=jax.ShapeDtypeStruct((rows, snps + width), jnp.float32),
        in_specs=[pl.BlockSpec((CROSS, width), lambda i: (i, 0)), pl.BlockSpec(pcs.shape, lambda i: (0, 0))],
        out_specs=pl.BlockSpec((rows, snps + width), lambda i: (0, 0)),
        compiler_params=pltpu.CompilerParams(vmem_limit_bytes=FRONT_BYTES),
        cost_estimate=FREE,
    )(genotypes, pcs)


def coef_kernel(cuts, pair_ref, got_ref, coef_ref, own_ref, near_ref, late_ref):
    rows, (snps, width) = pair_ref.shape[0], (coef_ref.shape[1], near_ref.shape[1])
    across_lanes = (((1,), (1,)), ((), ()))
    cross = pair_ref[:, :snps] + got_ref[:, :snps]
    gram = jnp.zeros((rows, rows), jnp.float32)
    blank = jnp.zeros((PAD - rows, width), jnp.float32)
    for j, ref in enumerate((pair_ref, pair_ref, got_ref, got_ref)):
        design = ref[:, snps + j % 2 * width:snps + (j % 2 + 1) * width]
        gram = gram + lax.dot_general(design, design, across_lanes, precision=HIGH, preferred_element_type=jnp.float32)
        if j > 0:
            design = jnp.concatenate([design[:, at:at + n] for first, n in cuts for at in (first, first + width // 2)], axis=1)
        stacked = right_stack(jnp.concatenate([design, blank], axis=0))
        if j < 2:
            (own_ref, near_ref)[j][...] = stacked
        else:
            late_ref[j - 2] = stacked
    row = lax.broadcasted_iota(jnp.int32, (rows, rows), 0)
    unit = (row == lax.broadcasted_iota(jnp.int32, (rows, rows), 1)).astype(jnp.float32)
    gram = gram + jnp.where(row >= DESIGN_ROWS, unit, 0.0)
    left, inverse = gram, unit
    for j in range(DESIGN_ROWS):
        pivot = 1.0 / left[j:j + 1, j:j + 1]
        factor = (left[:, j:j + 1] - unit[:, j:j + 1]) * pivot
        left, inverse = left - factor * left[j:j + 1, :], inverse - factor * inverse[j:j + 1, :]
    coef = jnp.dot(inverse, cross, precision=HIGH, preferred_element_type=jnp.float32)
    rest = cross - jnp.dot(gram, coef, precision=HIGH, preferred_element_type=jnp.float32)
    coef = coef + jnp.dot(inverse, rest, precision=HIGH, preferred_element_type=jnp.float32)
    coef_ref[...] = left_stack(jnp.concatenate([coef, jnp.zeros((PAD - rows, snps), jnp.float32)], axis=0))


def coefficients(pair, got, snps, cuts):
    vmem = pl.BlockSpec(memory_space=pltpu.VMEM)
    width = (pair.shape[1] - snps) // 2
    shapes = [(6 * PAD, snps), (6 * PAD, width), (6 * PAD, width), (2, 6 * PAD, width)]
    return pl.pallas_call(
        functools.partial(coef_kernel, cuts),
        out_shape=tuple(jax.ShapeDtypeStruct(shape, jnp.bfloat16) for shape in shapes),
        in_specs=[vmem] * 2,
        out_specs=(vmem,) * 4,
        compiler_params=pltpu.CompilerParams(vmem_limit_bytes=VMEM_BYTES),
        cost_estimate=pl.CostEstimate(flops=10**10, bytes_accessed=0, transcendentals=0),
    )(pair, got)


def pack(sums):
    size = jnp.exp2(8.0 * jnp.log2(jnp.maximum(jnp.abs(sums), 1e-30)) + 20.0)
    return jnp.where(sums < 0.0, -size, size).astype(jnp.bfloat16)


def unpack(packed):
    value = packed.astype(jnp.float32)
    size = jnp.abs(value)
    sums = jnp.exp2(jnp.log2(jnp.where(size > 0.0, size, 1.0)) * 0.125 - 2.5)
    return jnp.where(size > 0.0, jnp.where(value < 0.0, -sums, sums), 0.0)


def own_kernel(place_ref, coef_ref, design_ref, own_ref, terms_ref, keep_ref, give_ref):
    half = keep_ref.shape[1]
    snps = coef_ref.shape[1]

    def terms(k, _):
        at = pl.ds(pl.multiple_of(k * STEP, STEP), STEP)
        dosage = own_ref[at, :]
        fitted = product(coef_ref[:, at], design_ref[...])
        terms_ref[0, at, :], terms_ref[1, at, :] = resid_spread(dosage, dosage >= 0.0, fitted)
        return 0

    lax.fori_loop(0, snps // STEP, terms, 0)
    first_core = place_ref[0] == 0
    for t in range(2):
        a, b = [product(terms_ref[t, :, h * half:(h + 1) * half], terms_ref[t]) for h in range(2)]
        keep_ref[t] = jnp.where(first_core, a, b)
        give_ref[t] = pack(jnp.where(first_core, b, a))


def block_kernel(groups, place_ref, coef_ref, design_ref, terms_ref, *refs):
    *coded, keep_ref, give_ref, rows_ref = refs
    snps = coef_ref.shape[1]

    def terms(k, _):
        at = pl.ds(pl.multiple_of(k * STEP, STEP), STEP)
        first = 0
        for choices, design, count, _ in groups:
            here = slice(first, first + 2 * count)
            values = [coded[i][at, c:c + 2 * count] for i, c in choices]
            value = values[0] if len(values) == 1 else jnp.where(place_ref[1] == 1, values[0], values[1])
            dosage, observed = decode(value)
            fitted = product(coef_ref[:, at], design_ref[design])
            rows_ref[0, at, here], rows_ref[1, at, here] = resid_spread(dosage, observed, fitted)
            first += 2 * count
        return 0

    lax.fori_loop(0, snps // STEP, terms, 0)
    first_core = place_ref[0] == 0
    first = 0
    for _, _, count, target in groups:
        for t in range(2):
            sums = product(rows_ref[t, :, first:first + 2 * count], terms_ref[t])
            a, b = sums[:count], sums[count:]
            keep_ref[target(t)] = jnp.where(first_core, a, b)
            give_ref[target(t)] = pack(jnp.where(first_core, b, a))
        first += 2 * count


def block_sums(place, coef, design, sums, own=None, terms=None, coded=(), groups=()):
    snps = coef.shape[1]
    vmem = pl.BlockSpec(memory_space=pltpu.VMEM)
    out = (jax.ShapeDtypeStruct(sums, jnp.float32), jax.ShapeDtypeStruct(sums, jnp.bfloat16))
    if own is not None:
        kernel, operands, scratch = own_kernel, (place, coef, design, own), []
        out = (jax.ShapeDtypeStruct((2,) + own.shape, jnp.bfloat16),) + out
    else:
        kernel, operands = functools.partial(block_kernel, groups), (place, coef, design, terms, *coded)
        scratch = [pltpu.VMEM((2, snps, sum(2 * group[2] for group in groups)), jnp.bfloat16)]
    return pl.pallas_call(
        kernel,
        out_shape=out,
        in_specs=[pl.BlockSpec(memory_space=pltpu.SMEM)] + [vmem] * (len(operands) - 1),
        out_specs=tuple(vmem for _ in out),
        scratch_shapes=scratch,
        compiler_params=pltpu.CompilerParams(vmem_limit_bytes=VMEM_BYTES),
        cost_estimate=FREE,
    )(*operands)


def add_kernel(first, place_ref, own_ref, near_ref, late_ref, got_own_ref, got_near_ref, got_late_ref, mine_ref, *refs):
    *sent, sums = refs
    here = slice(first, first + mine_ref.shape[1])
    sums[0] = own_ref[:, here] + unpack(got_own_ref[:, here])
    sums[1] = near_ref[:, here] + unpack(got_near_ref[:, here])
    for i in range(2):
        sums[2 + i] = late_ref[i] + unpack(got_late_ref[i])
    mine_ref[...] = sums[place_ref[2]]
    for d, ref in enumerate(sent, 1):
        ref[...] = pack(sums[jnp.bitwise_xor(place_ref[2], d)])


def add_cores(place, first, *operands):
    shape = operands[2].shape[1:]
    vmem = pl.BlockSpec(memory_space=pltpu.VMEM)
    return pl.pallas_call(
        functools.partial(add_kernel, first),
        out_shape=(jax.ShapeDtypeStruct(shape, jnp.float32),) + (jax.ShapeDtypeStruct(shape, jnp.bfloat16),) * 3,
        in_specs=[pl.BlockSpec(memory_space=pltpu.SMEM)] + [vmem] * len(operands),
        out_specs=(vmem,) * 4,
        scratch_shapes=[pltpu.VMEM((4,) + shape, jnp.float32)],
        compiler_params=pltpu.CompilerParams(vmem_limit_bytes=VMEM_BYTES),
        cost_estimate=FREE,
    )(place, *operands)


def divide_kernel(*refs):
    *parts, out_ref = refs
    parts = parts[len(parts) % 4:]
    first = 0
    for p in range(len(parts) // 4):
        mine, *got = parts[4 * p:4 * p + 4]
        count = mine.shape[1]
        sums = [mine[t] + unpack(got[0][t]) + unpack(got[1][t]) + unpack(got[2][t]) for t in range(2)]
        out_ref[first:first + count, :] = sums[0] / (4.0 * sums[1])
        first += count


def divide(parts, rows, first, before=()):
    count, width = sum(m.shape[1] for m in parts[::4]), parts[0].shape[2]
    return pl.pallas_call(
        divide_kernel,
        grid=(1,),
        out_shape=jax.ShapeDtypeStruct((rows, width), jnp.float32),
        in_specs=[pl.BlockSpec(memory_space=pl.ANY) for _ in before] + [pl.BlockSpec(x.shape, lambda i: (0, 0, 0)) for x in parts],
        out_specs=pl.BlockSpec((count, width), lambda i: (first // count, 0)),
        input_output_aliases={0: 0} if before else {},
        compiler_params=pltpu.CompilerParams(vmem_limit_bytes=VMEM_BYTES),
        cost_estimate=FREE,
    )(*before, *parts)


def kinship(sums):
    return sums[0] / (4.0 * sums[1])


def after(value, *earlier):
    return lax.optimization_barrier((value, *earlier))[0]


def line_of_four(genotypes, pcs):
    width = genotypes.shape[1]
    half = width // 2
    s = lax.axis_index("snp")
    z = lax.axis_index("samp")
    chip = lax.div(s, 2)
    inner = jnp.logical_or(z == 1, z == 2)
    place = jnp.stack([lax.rem(s, 2), inner.astype(jnp.int32), chip ^ z])
    other_core = [(i, i ^ 1) for i in range(8)]
    cuts, pieces = ((0, half // 2), (half // 2, half // 4), (3 * half // 4, half // 4)), ((0,), (1, 2))
    mine = cross_part(genotypes, pcs)
    snps = genotypes.shape[0]
    other = lax.ppermute(mine, "samp", [(i, i ^ 1) for i in range(4)])
    pair = jnp.concatenate([mine[:, :snps] + other[:, :snps], mine[:, snps:], other[:, snps:]], axis=1)
    got = lax.ppermute(pair, "samp", [(i, i ^ 2) for i in range(4)])
    coef, design_own, design_near, design_late = coefficients(pair, got, snps, cuts)

    coded = []
    for piece in pieces:
        columns = [genotypes[:, at:at + n] for p in piece for first, n in cuts[p:p + 1] for at in (first, first + half)]
        coded.append(encode(after(jnp.concatenate(columns, axis=1), mine if not coded else pair)))
    near = [lax.ppermute(c, "samp", [(i, i ^ 1) for i in range(4)]) for c in coded]
    across = [lax.ppermute(c, "samp", [(1, 2), (2, 1)]) for c in coded]
    held, begin = {}, {}
    for i, piece in enumerate(pieces):
        at = 0
        for p in piece:
            held[p] = (i, at)
            at += 2 * cuts[p][1]
    start = 0
    for p, (_, count) in enumerate(cuts):
        begin[p] = start
        start += 2 * count

    sums = (2, half, width)
    terms, keep_own, give_own = block_sums(place, coef, design_own, sums, own=genotypes)
    groups = [
        (((held[p]),), (slice(None), slice(begin[p], begin[p] + 2 * n)), n, lambda t, first=first, n=n: (t, slice(first, first + n)))
        for p, (first, n) in enumerate(cuts)
    ]
    keep_near, give_near = block_sums(place, coef, design_near, sums, terms=terms, coded=near, groups=groups)
    got_own, got_near = [lax.ppermute(g, "snp", other_core) for g in (give_own, give_near)]
    totals, gates = [], [(), (), ()]
    for p, (first, count) in enumerate(cuts):
        i, at = held[p]
        cols = slice(at, at + 2 * count)
        ready = jnp.where(inner, near[i][:, cols], coded[i][:, cols])
        again = across[i][:, cols]
        if gates[p]:
            ready, again = [after(r, *gates[p]) for r in (ready, again)]
        far = lax.ppermute(ready, "samp", [(1, 2), (2, 1), (0, 3), (3, 0)])
        out = lax.ppermute(again, "samp", [(1, 0), (2, 3)])
        where = [(g, slice(None), slice(begin[p], begin[p] + 2 * count)) for g in range(2)]
        groups = [
            (choices, where[g], count, lambda t, g=g: (g, t)) for g, choices in enumerate((((0, 0), (1, 0)), ((2, at), (0, 0))))
        ]
        if p == 2:
            terms = after(terms, *totals[1:4])
        keep, give = block_sums(place, coef, design_late, (2, 2, count, width), terms=terms, coded=(far, out, across[i]), groups=groups)
        got = lax.ppermute(give, "snp", other_core)
        kept, *sent = add_cores(place, first, keep_own, keep_near, keep, got_own, got_near, got)
        if p == 0:
            gates[2] = (kept,)
        totals.append(kept)
        for d in range(1, 4):
            totals.append(lax.ppermute(sent[d - 1], "snp", [(i, i ^ (2 * d)) for i in range(8)]))
    most = divide(totals[:-4], half, 0)
    return divide(totals[-4:], half, cuts[-1][0], (most,))


def any_mesh(genotypes, pcs):
    width = genotypes.shape[1]
    design = jnp.concatenate([jnp.ones((1, width), jnp.float32), pcs], axis=0)
    observed = genotypes >= 0.0
    dosage = jnp.where(observed, genotypes, 0.0)
    cross_part = lax.dot_general(design, dosage, (((1,), (1,)), ((), ())), precision=HIGH)
    cross = lax.psum(cross_part, "samp")
    full = lax.all_gather(design, "samp", axis=1, tiled=True)
    fitted = lax.dot_general(solve_coef(full, cross), design, OVER_ROWS, precision=HIGH)
    own = resid_spread(dosage, observed, fitted)
    rows = lax.all_gather(jnp.stack(own), "samp", axis=2, tiled=True)
    sums = jnp.stack([product(rows[t], own[t]) for t in range(2)])
    return kinship(lax.psum_scatter(sums, "snp", scatter_dimension=1, tiled=True))


def solution(mesh):
    body = line_of_four if (mesh.shape["snp"], mesh.shape["samp"]) == (8, 4) else any_mesh
    in_specs = (P("snp", "samp"), P(None, "samp"))
    return jax.shard_map(body, mesh=mesh, in_specs=in_specs, out_specs=P("snp", "samp"), check_vma=False)
```

```python
import functools

import jax
import jax.numpy as jnp
from jax import lax
from jax.experimental import pallas as pl
from jax.experimental.pallas import tpu as pltpu
from jax.sharding import PartitionSpec as P

HIGH = lax.Precision.HIGHEST
LINK = jnp.float16
OVER_ROWS = (((0,), (0,)), ((), ()))
RANGE = 120.0
PAD = 32
VMEM_BYTES = 24 * 2**20
FRONT_BYTES = 60 * 2**20
DESIGN_ROWS = 21
STEP = 1024
CROSS = 512
FREE = pl.CostEstimate(flops=0, bytes_accessed=0, transcendentals=0)


def solve_coef(design, cross):
    gram = jnp.dot(design, design.T, precision=HIGH)
    factor = jnp.linalg.cholesky(gram)
    return jax.scipy.linalg.cho_solve((factor, True), cross)


def encode(genotypes):
    return jnp.where(genotypes >= 0.0, jnp.exp2(RANGE * genotypes - RANGE), 0.0).astype(jnp.bfloat16)


def decode(coded):
    value = coded.astype(jnp.float32)
    observed = value > 0.0
    return jnp.log2(jnp.where(observed, value, 1.0)) * (1.0 / RANGE) + 1.0, observed


def thirds(x):
    a = x.astype(jnp.bfloat16)
    rest = x - a.astype(jnp.float32)
    b = rest.astype(jnp.bfloat16)
    return a, b, (rest - b.astype(jnp.float32)).astype(jnp.bfloat16)


def left_stack(x):
    a, b, c = thirds(x)
    return jnp.concatenate([a, a, b, b, a, c], axis=0)


def right_stack(y):
    a, b, c = thirds(y)
    return jnp.concatenate([a, b, a, b, c, a], axis=0)


def resid_spread(dosage, observed, fitted):
    twice = jnp.clip(fitted, 0.04, 1.96)
    product = twice * (2.0 - twice)
    resid = jnp.where(observed, dosage - twice, 0.0)
    spread = jnp.where(observed, 0.5 * jnp.sqrt(product), 0.0)
    return resid.astype(jnp.bfloat16), spread.astype(jnp.bfloat16)


def product(left, right):
    return lax.dot_general(left, right, OVER_ROWS, preferred_element_type=jnp.float32)


def cross_kernel(genotypes_ref, pcs_ref, mine_ref):
    count, width = genotypes_ref.shape
    k = pcs_ref.shape[0]
    rows = mine_ref.shape[0]
    snps = mine_ref.shape[1] - width
    genotypes = genotypes_ref[...]
    blank = jnp.zeros((rows - k - 1, width), jnp.float32)
    design = jnp.concatenate([jnp.ones((1, width), jnp.float32), pcs_ref[...], blank], axis=0)
    d = [t.astype(jnp.float32) for t in thirds(design)]
    stacked = jnp.concatenate(d + d[:1], axis=0).astype(jnp.bfloat16)
    g = thirds(jnp.where(genotypes >= 0.0, genotypes, 0.0))[:2]
    lanes = (((1,), (1,)), ((), ()))
    first, second = [lax.dot_general(t, stacked, lanes, preferred_element_type=jnp.float32) for t in g]
    cross = (first[:, 2 * rows:3 * rows] + second[:, rows:2 * rows]) + (first[:, rows:2 * rows] + second[:, :rows])
    cross = cross + first[:, :rows]
    step = pl.program_id(0)
    mine_ref[:, pl.ds(pl.multiple_of(step * count, count), count)] = cross.T

    @pl.when(step == 0)
    def _():
        mine_ref[:, snps:] = design


def cross_part(genotypes, pcs):
    snps, width = genotypes.shape
    rows = DESIGN_ROWS + -DESIGN_ROWS % 8
    return pl.pallas_call(
        cross_kernel,
        grid=(snps // CROSS,),
        out_shape=jax.ShapeDtypeStruct((rows, snps + width), jnp.float32),
        in_specs=[pl.BlockSpec((CROSS, width), lambda i: (i, 0)), pl.BlockSpec(pcs.shape, lambda i: (0, 0))],
        out_specs=pl.BlockSpec((rows, snps + width), lambda i: (0, 0)),
        compiler_params=pltpu.CompilerParams(vmem_limit_bytes=FRONT_BYTES),
        cost_estimate=FREE,
    )(genotypes, pcs)


def coef_kernel(cuts, pair_ref, got_ref, coef_ref, own_ref, near_ref, late_ref):
    rows, (snps, width) = pair_ref.shape[0], (coef_ref.shape[1], near_ref.shape[1])
    across_lanes = (((1,), (1,)), ((), ()))
    cross = pair_ref[:, :snps] + got_ref[:, :snps]
    gram = jnp.zeros((rows, rows), jnp.float32)
    blank = jnp.zeros((PAD - rows, width), jnp.float32)
    for j, ref in enumerate((pair_ref, pair_ref, got_ref, got_ref)):
        design = ref[:, snps + j % 2 * width:snps + (j % 2 + 1) * width]
        gram = gram + lax.dot_general(design, design, across_lanes, precision=HIGH, preferred_element_type=jnp.float32)
        if j > 0:
            design = jnp.concatenate([design[:, at:at + n] for first, n in cuts for at in (first, first + width // 2)], axis=1)
        stacked = right_stack(jnp.concatenate([design, blank], axis=0))
        if j < 2:
            (own_ref, near_ref)[j][...] = stacked
        else:
            late_ref[j - 2] = stacked
    row = lax.broadcasted_iota(jnp.int32, (rows, rows), 0)
    unit = (row == lax.broadcasted_iota(jnp.int32, (rows, rows), 1)).astype(jnp.float32)
    gram = gram + jnp.where(row >= DESIGN_ROWS, unit, 0.0)
    left, inverse = gram, unit
    for j in range(DESIGN_ROWS):
        pivot = 1.0 / left[j:j + 1, j:j + 1]
        factor = (left[:, j:j + 1] - unit[:, j:j + 1]) * pivot
        left, inverse = left - factor * left[j:j + 1, :], inverse - factor * inverse[j:j + 1, :]
    coef = jnp.dot(inverse, cross, precision=HIGH, preferred_element_type=jnp.float32)
    rest = cross - jnp.dot(gram, coef, precision=HIGH, preferred_element_type=jnp.float32)
    coef = coef + jnp.dot(inverse, rest, precision=HIGH, preferred_element_type=jnp.float32)
    coef_ref[...] = left_stack(jnp.concatenate([coef, jnp.zeros((PAD - rows, snps), jnp.float32)], axis=0))


def coefficients(pair, got, snps, cuts):
    vmem = pl.BlockSpec(memory_space=pltpu.VMEM)
    width = (pair.shape[1] - snps) // 2
    shapes = [(6 * PAD, snps), (6 * PAD, width), (6 * PAD, width), (2, 6 * PAD, width)]
    return pl.pallas_call(
        functools.partial(coef_kernel, cuts),
        out_shape=tuple(jax.ShapeDtypeStruct(shape, jnp.bfloat16) for shape in shapes),
        in_specs=[vmem] * 2,
        out_specs=(vmem,) * 4,
        compiler_params=pltpu.CompilerParams(vmem_limit_bytes=VMEM_BYTES),
        cost_estimate=pl.CostEstimate(flops=10**10, bytes_accessed=0, transcendentals=0),
    )(pair, got)


def pack(sums):
    size = jnp.exp2(8.0 * jnp.log2(jnp.maximum(jnp.abs(sums), 1e-30)) + 20.0)
    return jnp.where(sums < 0.0, -size, size).astype(jnp.bfloat16)


def unpack(packed):
    value = packed.astype(jnp.float32)
    size = jnp.abs(value)
    sums = jnp.exp2(jnp.log2(jnp.where(size > 0.0, size, 1.0)) * 0.125 - 2.5)
    return jnp.where(size > 0.0, jnp.where(value < 0.0, -sums, sums), 0.0)


def own_kernel(place_ref, coef_ref, design_ref, own_ref, terms_ref, keep_ref, give_ref):
    half = keep_ref.shape[1]
    snps = coef_ref.shape[1]

    def terms(k, _):
        at = pl.ds(pl.multiple_of(k * STEP, STEP), STEP)
        dosage = own_ref[at, :]
        fitted = product(coef_ref[:, at], design_ref[...])
        terms_ref[0, at, :], terms_ref[1, at, :] = resid_spread(dosage, dosage >= 0.0, fitted)
        return 0

    lax.fori_loop(0, snps // STEP, terms, 0)
    first_core = place_ref[0] == 0
    for t in range(2):
        a, b = [product(terms_ref[t, :, h * half:(h + 1) * half], terms_ref[t]) for h in range(2)]
        keep_ref[t] = jnp.where(first_core, a, b)
        give_ref[t] = pack(jnp.where(first_core, b, a))


def block_kernel(groups, place_ref, coef_ref, design_ref, terms_ref, *refs):
    *coded, keep_ref, give_ref, rows_ref = refs
    snps = coef_ref.shape[1]

    def terms(k, _):
        at = pl.ds(pl.multiple_of(k * STEP, STEP), STEP)
        first = 0
        for choices, design, count, _ in groups:
            here = slice(first, first + 2 * count)
            values = [coded[i][at, c:c + 2 * count] for i, c in choices]
            value = values[0] if len(values) == 1 else jnp.where(place_ref[1] == 1, values[0], values[1])
            dosage, observed = decode(value)
            fitted = product(coef_ref[:, at], design_ref[design])
            rows_ref[0, at, here], rows_ref[1, at, here] = resid_spread(dosage, observed, fitted)
            first += 2 * count
        return 0

    lax.fori_loop(0, snps // STEP, terms, 0)
    first_core = place_ref[0] == 0
    first = 0
    for _, _, count, target in groups:
        for t in range(2):
            sums = product(rows_ref[t, :, first:first + 2 * count], terms_ref[t])
            a, b = sums[:count], sums[count:]
            keep_ref[target(t)] = jnp.where(first_core, a, b)
            give_ref[target(t)] = pack(jnp.where(first_core, b, a))
        first += 2 * count


def block_sums(place, coef, design, sums, own=None, terms=None, coded=(), groups=()):
    snps = coef.shape[1]
    vmem = pl.BlockSpec(memory_space=pltpu.VMEM)
    out = (jax.ShapeDtypeStruct(sums, jnp.float32), jax.ShapeDtypeStruct(sums, jnp.bfloat16))
    if own is not None:
        kernel, operands, scratch = own_kernel, (place, coef, design, own), []
        out = (jax.ShapeDtypeStruct((2,) + own.shape, jnp.bfloat16),) + out
    else:
        kernel, operands = functools.partial(block_kernel, groups), (place, coef, design, terms, *coded)
        scratch = [pltpu.VMEM((2, snps, sum(2 * group[2] for group in groups)), jnp.bfloat16)]
    return pl.pallas_call(
        kernel,
        out_shape=out,
        in_specs=[pl.BlockSpec(memory_space=pltpu.SMEM)] + [vmem] * (len(operands) - 1),
        out_specs=tuple(vmem for _ in out),
        scratch_shapes=scratch,
        compiler_params=pltpu.CompilerParams(vmem_limit_bytes=VMEM_BYTES),
        cost_estimate=FREE,
    )(*operands)


def add_kernel(first, place_ref, own_ref, near_ref, late_ref, got_own_ref, got_near_ref, got_late_ref, mine_ref, *refs):
    *sent, sums = refs
    here = slice(first, first + mine_ref.shape[1])
    sums[0] = own_ref[:, here] + unpack(got_own_ref[:, here])
    sums[1] = near_ref[:, here] + unpack(got_near_ref[:, here])
    for i in range(2):
        sums[2 + i] = late_ref[i] + unpack(got_late_ref[i])
    mine_ref[...] = sums[place_ref[2]]
    for d, ref in enumerate(sent, 1):
        ref[...] = pack(sums[jnp.bitwise_xor(place_ref[2], d)])


def add_cores(place, first, *operands):
    shape = operands[2].shape[1:]
    vmem = pl.BlockSpec(memory_space=pltpu.VMEM)
    return pl.pallas_call(
        functools.partial(add_kernel, first),
        out_shape=(jax.ShapeDtypeStruct(shape, jnp.float32),) + (jax.ShapeDtypeStruct(shape, jnp.bfloat16),) * 3,
        in_specs=[pl.BlockSpec(memory_space=pltpu.SMEM)] + [vmem] * len(operands),
        out_specs=(vmem,) * 4,
        scratch_shapes=[pltpu.VMEM((4,) + shape, jnp.float32)],
        compiler_params=pltpu.CompilerParams(vmem_limit_bytes=VMEM_BYTES),
        cost_estimate=FREE,
    )(place, *operands)


def divide_kernel(*refs):
    *parts, out_ref = refs
    parts = parts[len(parts) % 4:]
    first = 0
    for p in range(len(parts) // 4):
        mine, *got = parts[4 * p:4 * p + 4]
        count = mine.shape[1]
        sums = [mine[t] + unpack(got[0][t]) + unpack(got[1][t]) + unpack(got[2][t]) for t in range(2)]
        out_ref[first:first + count, :] = sums[0] / (4.0 * sums[1])
        first += count


def divide(parts, rows, first, before=()):
    count, width = sum(m.shape[1] for m in parts[::4]), parts[0].shape[2]
    return pl.pallas_call(
        divide_kernel,
        grid=(1,),
        out_shape=jax.ShapeDtypeStruct((rows, width), jnp.float32),
        in_specs=[pl.BlockSpec(memory_space=pl.ANY) for _ in before] + [pl.BlockSpec(x.shape, lambda i: (0, 0, 0)) for x in parts],
        out_specs=pl.BlockSpec((count, width), lambda i: (first // count, 0)),
        input_output_aliases={0: 0} if before else {},
        compiler_params=pltpu.CompilerParams(vmem_limit_bytes=VMEM_BYTES),
        cost_estimate=FREE,
    )(*before, *parts)


def kinship(sums):
    return sums[0] / (4.0 * sums[1])


def after(value, *earlier):
    return lax.optimization_barrier((value, *earlier))[0]


def line_of_four(genotypes, pcs):
    width = genotypes.shape[1]
    half = width // 2
    s = lax.axis_index("snp")
    z = lax.axis_index("samp")
    chip = lax.div(s, 2)
    inner = jnp.logical_or(z == 1, z == 2)
    place = jnp.stack([lax.rem(s, 2), inner.astype(jnp.int32), chip ^ z])
    other_core = [(i, i ^ 1) for i in range(8)]
    cuts, pieces = ((0, half // 2), (half // 2, half // 4), (3 * half // 4, half // 4)), ((0,), (1, 2))
    mine = cross_part(genotypes, pcs)
    snps = genotypes.shape[0]
    other = lax.ppermute(mine, "samp", [(i, i ^ 1) for i in range(4)])
    pair = jnp.concatenate([mine[:, :snps] + other[:, :snps], mine[:, snps:], other[:, snps:]], axis=1)
    got = lax.ppermute(pair, "samp", [(i, i ^ 2) for i in range(4)])
    coef, design_own, design_near, design_late = coefficients(pair, got, snps, cuts)

    coded = []
    for piece in pieces:
        columns = [genotypes[:, at:at + n] for p in piece for first, n in cuts[p:p + 1] for at in (first, first + half)]
        coded.append(encode(after(jnp.concatenate(columns, axis=1), mine if not coded else pair)))
    near = [lax.ppermute(c, "samp", [(i, i ^ 1) for i in range(4)]) for c in coded]
    across = [lax.ppermute(c, "samp", [(1, 2), (2, 1)]) for c in coded]
    held, begin = {}, {}
    for i, piece in enumerate(pieces):
        at = 0
        for p in piece:
            held[p] = (i, at)
            at += 2 * cuts[p][1]
    start = 0
    for p, (_, count) in enumerate(cuts):
        begin[p] = start
        start += 2 * count

    sums = (2, half, width)
    terms, keep_own, give_own = block_sums(place, coef, design_own, sums, own=genotypes)
    groups = [
        (((held[p]),), (slice(None), slice(begin[p], begin[p] + 2 * n)), n, lambda t, first=first, n=n: (t, slice(first, first + n)))
        for p, (first, n) in enumerate(cuts)
    ]
    keep_near, give_near = block_sums(place, coef, design_near, sums, terms=terms, coded=near, groups=groups)
    got_own, got_near = [lax.ppermute(g, "snp", other_core) for g in (give_own, give_near)]
    totals, gates = [], [(), (), ()]
    for p, (first, count) in enumerate(cuts):
        i, at = held[p]
        cols = slice(at, at + 2 * count)
        ready = jnp.where(inner, near[i][:, cols], coded[i][:, cols])
        again = across[i][:, cols]
        if gates[p]:
            ready, again = [after(r, *gates[p]) for r in (ready, again)]
        far = lax.ppermute(ready, "samp", [(1, 2), (2, 1), (0, 3), (3, 0)])
        out = lax.ppermute(again, "samp", [(1, 0), (2, 3)])
        where = [(g, slice(None), slice(begin[p], begin[p] + 2 * count)) for g in range(2)]
        groups = [
            (choices, where[g], count, lambda t, g=g: (g, t)) for g, choices in enumerate((((0, 0), (1, 0)), ((2, at), (0, 0))))
        ]
        if p == 2:
            terms = after(terms, *totals[1:4])
        keep, give = block_sums(place, coef, design_late, (2, 2, count, width), terms=terms, coded=(far, out, across[i]), groups=groups)
        got = lax.ppermute(give, "snp", other_core)
        kept, *sent = add_cores(place, first, keep_own, keep_near, keep, got_own, got_near, got)
        if p == 0:
            gates[2] = (kept,)
        totals.append(kept)
        for d in range(1, 4):
            totals.append(lax.ppermute(sent[d - 1], "snp", [(i, i ^ (2 * d)) for i in range(8)]))
    most = divide(totals[:-4], half, 0)
    return divide(totals[-4:], half, cuts[-1][0], (most,))


def any_mesh(genotypes, pcs):
    width = genotypes.shape[1]
    design = jnp.concatenate([jnp.ones((1, width), jnp.float32), pcs], axis=0)
    observed = genotypes >= 0.0
    dosage = jnp.where(observed, genotypes, 0.0)
    cross_part = lax.dot_general(design, dosage, (((1,), (1,)), ((), ())), precision=HIGH)
    cross = lax.psum(cross_part, "samp")
    full = lax.all_gather(design, "samp", axis=1, tiled=True)
    fitted = lax.dot_general(solve_coef(full, cross), design, OVER_ROWS, precision=HIGH)
    own = resid_spread(dosage, observed, fitted)
    rows = lax.all_gather(jnp.stack(own), "samp", axis=2, tiled=True)
    sums = jnp.stack([product(rows[t], own[t]) for t in range(2)])
    return kinship(lax.psum_scatter(sums, "snp", scatter_dimension=1, tiled=True))


def solution(mesh):
    def body(genotypes, pcs):
        snps, width = genotypes.shape
        fits = (mesh.shape["snp"], mesh.shape["samp"]) == (8, 4) and snps % STEP == 0 and width % 512 == 0
        return (line_of_four if fits else any_mesh)(genotypes, pcs)

    in_specs = (P("snp", "samp"), P(None, "samp"))
    return jax.shard_map(body, mesh=mesh, in_specs=in_specs, out_specs=P("snp", "samp"), check_vma=False)
```

```python
import functools

import jax
import jax.numpy as jnp
from jax import lax
from jax.experimental import pallas as pl
from jax.experimental.pallas import tpu as pltpu
from jax.sharding import PartitionSpec as P

HIGH = lax.Precision.HIGHEST
LINK = jnp.float16
OVER_ROWS = (((0,), (0,)), ((), ()))
RANGE = 120.0
PAD = 32
VMEM_BYTES = 24 * 2**20
FRONT_BYTES = 60 * 2**20
DESIGN_ROWS = 21
STEP = 1024
CROSS = 512
FREE = pl.CostEstimate(flops=0, bytes_accessed=0, transcendentals=0)


def solve_coef(design, cross):
    gram = jnp.dot(design, design.T, precision=HIGH)
    factor = jnp.linalg.cholesky(gram)
    return jax.scipy.linalg.cho_solve((factor, True), cross)


def encode(genotypes):
    return jnp.where(genotypes >= 0.0, jnp.exp2(RANGE * genotypes - RANGE), 0.0).astype(jnp.bfloat16)


def decode(coded):
    value = coded.astype(jnp.float32)
    observed = value > 0.0
    return jnp.log2(jnp.where(observed, value, 1.0)) * (1.0 / RANGE) + 1.0, observed


def thirds(x):
    a = x.astype(jnp.bfloat16)
    rest = x - a.astype(jnp.float32)
    b = rest.astype(jnp.bfloat16)
    return a, b, (rest - b.astype(jnp.float32)).astype(jnp.bfloat16)


def left_stack(x):
    a, b, c = thirds(x)
    return jnp.concatenate([a, a, b, b, a, c], axis=0)


def right_stack(y):
    a, b, c = thirds(y)
    return jnp.concatenate([a, b, a, b, c, a], axis=0)


def resid_spread(dosage, observed, fitted):
    twice = jnp.clip(fitted, 0.04, 1.96)
    product = twice * (2.0 - twice)
    resid = jnp.where(observed, dosage - twice, 0.0)
    spread = jnp.where(observed, 0.5 * jnp.sqrt(product), 0.0)
    return resid.astype(jnp.bfloat16), spread.astype(jnp.bfloat16)


def product(left, right):
    return lax.dot_general(left, right, OVER_ROWS, preferred_element_type=jnp.float32)


def cross_kernel(columns, genotypes_ref, pcs_ref, mine_ref, coded_ref):
    count, width = genotypes_ref.shape
    k = pcs_ref.shape[0]
    rows = mine_ref.shape[0]
    snps = mine_ref.shape[1] - width
    genotypes = genotypes_ref[...]
    coded_ref[...] = encode(jnp.concatenate([genotypes[:, at:at + n] for at, n in columns], axis=1))
    blank = jnp.zeros((rows - k - 1, width), jnp.float32)
    design = jnp.concatenate([jnp.ones((1, width), jnp.float32), pcs_ref[...], blank], axis=0)
    d = [t.astype(jnp.float32) for t in thirds(design)]
    stacked = jnp.concatenate(d + d[:1], axis=0).astype(jnp.bfloat16)
    g = thirds(jnp.where(genotypes >= 0.0, genotypes, 0.0))[:2]
    lanes = (((1,), (1,)), ((), ()))
    first, second = [lax.dot_general(t, stacked, lanes, preferred_element_type=jnp.float32) for t in g]
    cross = (first[:, 2 * rows:3 * rows] + second[:, rows:2 * rows]) + (first[:, rows:2 * rows] + second[:, :rows])
    cross = cross + first[:, :rows]
    step = pl.program_id(0)
    mine_ref[:, pl.ds(pl.multiple_of(step * count, count), count)] = cross.T

    @pl.when(step == 0)
    def _():
        mine_ref[:, snps:] = design


def cross_part(genotypes, pcs, columns):
    snps, width = genotypes.shape
    size = sum(n for _, n in columns)
    rows = DESIGN_ROWS + -DESIGN_ROWS % 8
    return pl.pallas_call(
        functools.partial(cross_kernel, columns),
        grid=(snps // CROSS,),
        out_shape=(jax.ShapeDtypeStruct((rows, snps + width), jnp.float32), jax.ShapeDtypeStruct((snps, size), jnp.bfloat16)),
        in_specs=[pl.BlockSpec((CROSS, width), lambda i: (i, 0)), pl.BlockSpec(pcs.shape, lambda i: (0, 0))],
        out_specs=(pl.BlockSpec((rows, snps + width), lambda i: (0, 0)), pl.BlockSpec((CROSS, size), lambda i: (i, 0))),
        compiler_params=pltpu.CompilerParams(vmem_limit_bytes=FRONT_BYTES),
        cost_estimate=FREE,
    )(genotypes, pcs)


def coef_kernel(cuts, pair_ref, got_ref, coef_ref, own_ref, near_ref, late_ref):
    rows, (snps, width) = pair_ref.shape[0], (coef_ref.shape[1], near_ref.shape[1])
    across_lanes = (((1,), (1,)), ((), ()))
    cross = pair_ref[:, :snps] + got_ref[:, :snps]
    gram = jnp.zeros((rows, rows), jnp.float32)
    blank = jnp.zeros((PAD - rows, width), jnp.float32)
    for j, ref in enumerate((pair_ref, pair_ref, got_ref, got_ref)):
        design = ref[:, snps + j % 2 * width:snps + (j % 2 + 1) * width]
        gram = gram + lax.dot_general(design, design, across_lanes, precision=HIGH, preferred_element_type=jnp.float32)
        if j > 0:
            design = jnp.concatenate([design[:, at:at + n] for first, n in cuts for at in (first, first + width // 2)], axis=1)
        stacked = right_stack(jnp.concatenate([design, blank], axis=0))
        if j < 2:
            (own_ref, near_ref)[j][...] = stacked
        else:
            late_ref[j - 2] = stacked
    row = lax.broadcasted_iota(jnp.int32, (rows, rows), 0)
    unit = (row == lax.broadcasted_iota(jnp.int32, (rows, rows), 1)).astype(jnp.float32)
    gram = gram + jnp.where(row >= DESIGN_ROWS, unit, 0.0)
    left, inverse = gram, unit
    for j in range(DESIGN_ROWS):
        pivot = 1.0 / left[j:j + 1, j:j + 1]
        factor = (left[:, j:j + 1] - unit[:, j:j + 1]) * pivot
        left, inverse = left - factor * left[j:j + 1, :], inverse - factor * inverse[j:j + 1, :]
    coef = jnp.dot(inverse, cross, precision=HIGH, preferred_element_type=jnp.float32)
    rest = cross - jnp.dot(gram, coef, precision=HIGH, preferred_element_type=jnp.float32)
    coef = coef + jnp.dot(inverse, rest, precision=HIGH, preferred_element_type=jnp.float32)
    coef_ref[...] = left_stack(jnp.concatenate([coef, jnp.zeros((PAD - rows, snps), jnp.float32)], axis=0))


def coefficients(pair, got, snps, cuts):
    vmem = pl.BlockSpec(memory_space=pltpu.VMEM)
    width = (pair.shape[1] - snps) // 2
    shapes = [(6 * PAD, snps), (6 * PAD, width), (6 * PAD, width), (2, 6 * PAD, width)]
    return pl.pallas_call(
        functools.partial(coef_kernel, cuts),
        out_shape=tuple(jax.ShapeDtypeStruct(shape, jnp.bfloat16) for shape in shapes),
        in_specs=[vmem] * 2,
        out_specs=(vmem,) * 4,
        compiler_params=pltpu.CompilerParams(vmem_limit_bytes=VMEM_BYTES),
        cost_estimate=pl.CostEstimate(flops=10**11, bytes_accessed=0, transcendentals=0),
    )(pair, got)


def pack(sums):
    size = jnp.exp2(8.0 * jnp.log2(jnp.maximum(jnp.abs(sums), 1e-30)) + 20.0)
    return jnp.where(sums < 0.0, -size, size).astype(jnp.bfloat16)


def unpack(packed):
    value = packed.astype(jnp.float32)
    size = jnp.abs(value)
    sums = jnp.exp2(jnp.log2(jnp.where(size > 0.0, size, 1.0)) * 0.125 - 2.5)
    return jnp.where(size > 0.0, jnp.where(value < 0.0, -sums, sums), 0.0)


def own_kernel(place_ref, coef_ref, design_ref, own_ref, terms_ref, keep_ref, give_ref):
    half = keep_ref.shape[1]
    snps = coef_ref.shape[1]

    def terms(k, _):
        at = pl.ds(pl.multiple_of(k * STEP, STEP), STEP)
        dosage = own_ref[at, :]
        fitted = product(coef_ref[:, at], design_ref[...])
        terms_ref[0, at, :], terms_ref[1, at, :] = resid_spread(dosage, dosage >= 0.0, fitted)
        return 0

    lax.fori_loop(0, snps // STEP, terms, 0)
    first_core = place_ref[0] == 0
    for t in range(2):
        a, b = [product(terms_ref[t, :, h * half:(h + 1) * half], terms_ref[t]) for h in range(2)]
        keep_ref[t] = jnp.where(first_core, a, b)
        give_ref[t] = pack(jnp.where(first_core, b, a))


def block_kernel(groups, place_ref, coef_ref, design_ref, terms_ref, *refs):
    *coded, keep_ref, give_ref, rows_ref = refs
    snps = coef_ref.shape[1]

    def terms(k, _):
        at = pl.ds(pl.multiple_of(k * STEP, STEP), STEP)
        first = 0
        for choices, design, count, _ in groups:
            here = slice(first, first + 2 * count)
            values = [coded[i][at, c:c + 2 * count] for i, c in choices]
            value = values[0] if len(values) == 1 else jnp.where(place_ref[1] == 1, values[0], values[1])
            dosage, observed = decode(value)
            fitted = product(coef_ref[:, at], design_ref[design])
            rows_ref[0, at, here], rows_ref[1, at, here] = resid_spread(dosage, observed, fitted)
            first += 2 * count
        return 0

    lax.fori_loop(0, snps // STEP, terms, 0)
    first_core = place_ref[0] == 0
    first = 0
    for _, _, count, target in groups:
        for t in range(2):
            sums = product(rows_ref[t, :, first:first + 2 * count], terms_ref[t])
            a, b = sums[:count], sums[count:]
            keep_ref[target(t)] = jnp.where(first_core, a, b)
            give_ref[target(t)] = pack(jnp.where(first_core, b, a))
        first += 2 * count


def block_sums(place, coef, design, sums, own=None, terms=None, coded=(), groups=()):
    snps = coef.shape[1]
    vmem = pl.BlockSpec(memory_space=pltpu.VMEM)
    out = (jax.ShapeDtypeStruct(sums, jnp.float32), jax.ShapeDtypeStruct(sums, jnp.bfloat16))
    if own is not None:
        kernel, operands, scratch = own_kernel, (place, coef, design, own), []
        out = (jax.ShapeDtypeStruct((2,) + own.shape, jnp.bfloat16),) + out
    else:
        kernel, operands = functools.partial(block_kernel, groups), (place, coef, design, terms, *coded)
        scratch = [pltpu.VMEM((2, snps, sum(2 * group[2] for group in groups)), jnp.bfloat16)]
    return pl.pallas_call(
        kernel,
        out_shape=out,
        in_specs=[pl.BlockSpec(memory_space=pltpu.SMEM)] + [vmem] * (len(operands) - 1),
        out_specs=tuple(vmem for _ in out),
        scratch_shapes=scratch,
        compiler_params=pltpu.CompilerParams(vmem_limit_bytes=VMEM_BYTES),
        cost_estimate=FREE,
    )(*operands)


def add_kernel(first, place_ref, own_ref, near_ref, late_ref, got_own_ref, got_near_ref, got_late_ref, mine_ref, *refs):
    *sent, sums = refs
    here = slice(first, first + mine_ref.shape[1])
    sums[0] = own_ref[:, here] + unpack(got_own_ref[:, here])
    sums[1] = near_ref[:, here] + unpack(got_near_ref[:, here])
    for i in range(2):
        sums[2 + i] = late_ref[i] + unpack(got_late_ref[i])
    mine_ref[...] = sums[place_ref[2]]
    for d, ref in enumerate(sent, 1):
        ref[...] = pack(sums[jnp.bitwise_xor(place_ref[2], d)])


def add_cores(place, first, *operands):
    shape = operands[2].shape[1:]
    vmem = pl.BlockSpec(memory_space=pltpu.VMEM)
    return pl.pallas_call(
        functools.partial(add_kernel, first),
        out_shape=(jax.ShapeDtypeStruct(shape, jnp.float32),) + (jax.ShapeDtypeStruct(shape, jnp.bfloat16),) * 3,
        in_specs=[pl.BlockSpec(memory_space=pltpu.SMEM)] + [vmem] * len(operands),
        out_specs=(vmem,) * 4,
        scratch_shapes=[pltpu.VMEM((4,) + shape, jnp.float32)],
        compiler_params=pltpu.CompilerParams(vmem_limit_bytes=VMEM_BYTES),
        cost_estimate=FREE,
    )(place, *operands)


def divide_kernel(*refs):
    *parts, out_ref = refs
    parts = parts[len(parts) % 4:]
    first = 0
    for p in range(len(parts) // 4):
        mine, *got = parts[4 * p:4 * p + 4]
        count = mine.shape[1]
        sums = [mine[t] + unpack(got[0][t]) + unpack(got[1][t]) + unpack(got[2][t]) for t in range(2)]
        out_ref[first:first + count, :] = sums[0] / (4.0 * sums[1])
        first += count


def divide(parts, rows, first, before=()):
    count, width = sum(m.shape[1] for m in parts[::4]), parts[0].shape[2]
    return pl.pallas_call(
        divide_kernel,
        grid=(1,),
        out_shape=jax.ShapeDtypeStruct((rows, width), jnp.float32),
        in_specs=[pl.BlockSpec(memory_space=pl.ANY) for _ in before] + [pl.BlockSpec(x.shape, lambda i: (0, 0, 0)) for x in parts],
        out_specs=pl.BlockSpec((count, width), lambda i: (first // count, 0)),
        input_output_aliases={0: 0} if before else {},
        compiler_params=pltpu.CompilerParams(vmem_limit_bytes=VMEM_BYTES),
        cost_estimate=FREE,
    )(*before, *parts)


def kinship(sums):
    return sums[0] / (4.0 * sums[1])


def after(value, *earlier):
    return lax.optimization_barrier((value, *earlier))[0]


def line_of_four(genotypes, pcs):
    width = genotypes.shape[1]
    half = width // 2
    s = lax.axis_index("snp")
    z = lax.axis_index("samp")
    chip = lax.div(s, 2)
    inner = jnp.logical_or(z == 1, z == 2)
    place = jnp.stack([lax.rem(s, 2), inner.astype(jnp.int32), chip ^ z])
    other_core = [(i, i ^ 1) for i in range(8)]
    cuts, pieces = ((0, half // 2), (half // 2, half // 4), (3 * half // 4, half // 4)), ((0,), (1, 2))
    columns = [[(at, n) for p in piece for first, n in cuts[p:p + 1] for at in (first, first + half)] for piece in pieces]
    mine, ahead = cross_part(genotypes, pcs, columns[0])
    snps = genotypes.shape[0]
    other = lax.ppermute(mine, "samp", [(i, i ^ 1) for i in range(4)])
    pair = jnp.concatenate([mine[:, :snps] + other[:, :snps], mine[:, snps:], other[:, snps:]], axis=1)
    got = lax.ppermute(pair, "samp", [(i, i ^ 2) for i in range(4)])
    coef, design_own, design_near, design_late = coefficients(pair, got, snps, cuts)

    rest = [jnp.concatenate([genotypes[:, at:at + n] for at, n in c], axis=1) for c in columns[1:]]
    coded = [after(ahead, mine)] + [encode(after(r, pair)) for r in rest]
    near = [lax.ppermute(c, "samp", [(i, i ^ 1) for i in range(4)]) for c in coded]
    across = [lax.ppermute(c, "samp", [(1, 2), (2, 1)]) for c in coded]
    held, begin = {}, {}
    for i, piece in enumerate(pieces):
        at = 0
        for p in piece:
            held[p] = (i, at)
            at += 2 * cuts[p][1]
    start = 0
    for p, (_, count) in enumerate(cuts):
        begin[p] = start
        start += 2 * count

    sums = (2, half, width)
    terms, keep_own, give_own = block_sums(place, coef, design_own, sums, own=genotypes)
    groups = [
        (((held[p]),), (slice(None), slice(begin[p], begin[p] + 2 * n)), n, lambda t, first=first, n=n: (t, slice(first, first + n)))
        for p, (first, n) in enumerate(cuts)
    ]
    keep_near, give_near = block_sums(place, coef, design_near, sums, terms=terms, coded=near, groups=groups)
    got_own, got_near = [lax.ppermute(g, "snp", other_core) for g in (give_own, give_near)]
    totals, gates = [], [(), (), ()]
    for p, (first, count) in enumerate(cuts):
        i, at = held[p]
        cols = slice(at, at + 2 * count)
        ready = jnp.where(inner, near[i][:, cols], coded[i][:, cols])
        again = across[i][:, cols]
        if gates[p]:
            ready, again = [after(r, *gates[p]) for r in (ready, again)]
        far = lax.ppermute(ready, "samp", [(1, 2), (2, 1), (0, 3), (3, 0)])
        out = lax.ppermute(again, "samp", [(1, 0), (2, 3)])
        where = [(g, slice(None), slice(begin[p], begin[p] + 2 * count)) for g in range(2)]
        groups = [
            (choices, where[g], count, lambda t, g=g: (g, t)) for g, choices in enumerate((((0, 0), (1, 0)), ((2, at), (0, 0))))
        ]
        if p == 2:
            terms = after(terms, *totals[1:4])
        keep, give = block_sums(place, coef, design_late, (2, 2, count, width), terms=terms, coded=(far, out, across[i]), groups=groups)
        got = lax.ppermute(give, "snp", other_core)
        kept, *sent = add_cores(place, first, keep_own, keep_near, keep, got_own, got_near, got)
        if p == 0:
            gates[2] = (kept,)
        totals.append(kept)
        for d in (3, 1, 2):
            totals.append(lax.ppermute(sent[d - 1], "snp", [(i, i ^ (2 * d)) for i in range(8)]))
    most = divide(totals[:-4], half, 0)
    return divide(totals[-4:], half, cuts[-1][0], (most,))


def any_mesh(genotypes, pcs):
    width = genotypes.shape[1]
    design = jnp.concatenate([jnp.ones((1, width), jnp.float32), pcs], axis=0)
    observed = genotypes >= 0.0
    dosage = jnp.where(observed, genotypes, 0.0)
    cross_part = lax.dot_general(design, dosage, (((1,), (1,)), ((), ())), precision=HIGH)
    cross = lax.psum(cross_part, "samp")
    full = lax.all_gather(design, "samp", axis=1, tiled=True)
    fitted = lax.dot_general(solve_coef(full, cross), design, OVER_ROWS, precision=HIGH)
    own = resid_spread(dosage, observed, fitted)
    rows = lax.all_gather(jnp.stack(own), "samp", axis=2, tiled=True)
    sums = jnp.stack([product(rows[t], own[t]) for t in range(2)])
    return kinship(lax.psum_scatter(sums, "snp", scatter_dimension=1, tiled=True))


def solution(mesh):
    def body(genotypes, pcs):
        snps, width = genotypes.shape
        fits = (mesh.shape["snp"], mesh.shape["samp"]) == (8, 4) and snps % STEP == 0 and width % 512 == 0
        return (line_of_four if fits else any_mesh)(genotypes, pcs)

    in_specs = (P("snp", "samp"), P(None, "samp"))
    return jax.shard_map(body, mesh=mesh, in_specs=in_specs, out_specs=P("snp", "samp"), check_vma=False)
```
